512 devices in a mesh: dom: 16 (over x, z_hi, core), slab: 32 (over y, z_lo).
Axes of the slice: x: 4, y: 8, z: 8 (z_hi: 2, z_lo: 4; z = z_hi * 4 + z_lo), core: 2. Of those that a mesh axis runs over, the one named last changes fastest.
Arguments:
- positions: float32 [3, 524288], P(None, ('dom', 'slab')), as said below
- features: bfloat16 [32, 524288], P(None, ('dom', 'slab')), may hold values from -6 to 6
- counts: int32 [512], P(('dom', 'slab')), may hold values from 512 to 1024, as said below
- ghost_index: int32 [512, 256], P(('dom', 'slab')), may hold values from 0 to 511, as said below
- kvec: int32 [3, 8192], replicated, may hold values from -12 to 12
- screen_len: float32 [32], replicated, may hold values from 2 to 20
- long_weight: bfloat16 [32, 32], replicated, may hold values from -1 to 1
- short_weight: bfloat16 [32, 32], replicated, may hold values from -1 to 1
Outputs:
- updated: bfloat16 [32, 524288], P(None, ('dom', 'slab'))
The draws below stay inside these ranges and needn't reach their ends.
Inputs may be any that keep to these rules, and one draw needn't show every extreme that they name: `counts`: at least one device is full (1024 live) and at least one holds exactly 512. `ghost_index`: Lower-face senders are distinct slots below 256; upper-face senders are distinct slots from 256 to 511; all are live. `positions`: each atom lies inside its block's domain and slab region of the box.
All inputs are finite; a program needn't handle non-finite values.
Results may differ from the reference program's by a relative error of at most 0.005.
The reference program's roundings to bfloat16 on the way (of `masked` and `pair`) count: a program that leaves them out, or rounds other values in their place, can miss the bound.
Values may be sent and summed in bfloat16 or wider, within the bound.
No kernel may reach another device: no remote copies, remote signals or barrier semaphores. Data moves between devices by JAX's collectives and lax.ppermute only.
A program may use at most 128 MiB of HBM per device.

```python
import math
import jax
import jax.numpy as jnp
from jax import lax

C = 32
K_VEC = 8192
ATOM_DEV = 1024
GHOST = 128
ATOMS = 524288
N_DOM = 16
N_SLAB = 32


box_length = 216.0


def draw_positions(key, part):
    key = jax.random.fold_in(key, 11)
    key_x, key_y, key_z = jax.random.split(key, 3)
    devices = N_DOM * N_SLAB
    width_x = box_length / N_DOM
    frac = min(4.0 / width_x, 0.5)
    slots = jnp.arange(ATOM_DEV)
    lower = (slots < 2 * GHOST)[None, :]
    upper = ((slots >= 2 * GHOST) & (slots < 4 * GHOST))[None, :]
    across = jax.random.uniform(key_x, (devices, ATOM_DEV), jnp.float32)
    across = jnp.where(lower, across * frac, jnp.where(upper, 1.0 - frac * across, across))
    owner = jnp.arange(devices)
    dom_pos = (owner // N_SLAB).astype(jnp.float32)
    slab_pos = (owner % N_SLAB).astype(jnp.float32)
    xcoord = (dom_pos[:, None] + across) * width_x
    ycoord = (slab_pos[:, None] + jax.random.uniform(key_y, (devices, ATOM_DEV), jnp.float32)) * (box_length / N_SLAB)
    zcoord = jax.random.uniform(key_z, (devices, ATOM_DEV), jnp.float32) * box_length
    return jnp.stack([xcoord, ycoord, zcoord]).reshape(3, devices * ATOM_DEV)


def draw_counts(key, part):
    key = jax.random.fold_in(key, 23)
    key_a, key_b = jax.random.split(key)
    devices = N_DOM * N_SLAB
    counts = jax.random.randint(key_a, (devices,), 4 * GHOST, ATOM_DEV + 1)
    order = jax.random.permutation(key_b, devices)
    counts = counts.at[order[0]].set(ATOM_DEV).at[order[1]].set(4 * GHOST)
    return counts.astype(jnp.int32)


def draw_ghost_index(key, part):
    key = jax.random.fold_in(key, 37)
    key_a, key_b = jax.random.split(key)
    devices = N_DOM * N_SLAB
    keys_low = jax.random.split(key_a, devices)
    keys_high = jax.random.split(key_b, devices)
    lows = jax.vmap(lambda k: jax.random.permutation(k, 2 * GHOST)[:GHOST])(keys_low)
    highs = jax.vmap(lambda k: jax.random.permutation(k, 2 * GHOST)[:GHOST])(keys_high) + 2 * GHOST
    return jnp.concatenate([lows, highs], axis=1).astype(jnp.int32)


def set_ends(drawn, own_key, low, largest):
    shape = drawn.shape
    place = [jax.random.randint(jax.random.fold_in(own_key, axis), (), 0, shape[axis]) for axis in range(len(shape))]
    drawn = drawn.at[tuple(place)].set(low)
    longest = shape.index(max(shape))
    place[longest] = (place[longest] + 1) % shape[longest]
    return drawn.at[tuple(place)].set(largest)


def level_of(rng, extent, cuts, smallest, top_value):
    def one(position, shards_of):
        steps = jax.random.uniform(jax.random.fold_in(jax.random.fold_in(rng, 6), position), (shards_of,), jnp.float32, smallest / len(cuts), top_value / len(cuts))
        return jnp.repeat(jnp.exp(steps), extent[position] // shards_of).reshape((-1,) + (1,) * (len(extent) - position - 1))

    factor_of = one(*cuts[0])
    for cut in cuts[1:]:
        factor_of = factor_of * one(*cut)
    return factor_of


def gaussian(stream_key, shape, spread, reach, pieces=(), kind=jnp.bfloat16):
    drawn = spread * jax.random.normal(stream_key, shape, jnp.float32)
    if pieces:
        drawn = drawn * level_of(stream_key, shape, pieces, -0.22, 0.18)
    return jnp.clip(drawn, -reach, reach).astype(kind)


def setup_inputs(seed: int = 0) -> dict:
    splits = jax.random.split(jax.random.key(seed), 9)
    positions = draw_positions(jax.random.fold_in(splits[8], 71), 0)
    features = gaussian(splits[1], (C, ATOMS), 1.0, 6.0, ((1, 512),))
    counts = draw_counts(jax.random.fold_in(splits[8], 71), 0)
    ghost_index = draw_ghost_index(jax.random.fold_in(splits[8], 71), 0)
    kvec = set_ends(jax.random.randint(splits[4], (3, K_VEC), -12, 13), jax.random.fold_in(splits[4], 1), -12, 12).astype(jnp.int32)
    screen_len = jnp.clip(jnp.exp(jax.random.uniform(splits[5], (C,), jnp.float32, math.log(2.0), math.log(20.0))), 2.0, 20.0)
    long_weight = gaussian(splits[6], (C, C), C ** -0.5, 1.0)
    short_weight = gaussian(splits[7], (C, C), C ** -0.5, 1.0)
    return {"positions": positions, "features": features, "counts": counts, "ghost_index": ghost_index, "kvec": kvec, "screen_len": screen_len, "long_weight": long_weight, "short_weight": short_weight}


box_length = 216.0
pair_scale = 12.5
short_gain = 0.5
long_gain = 16.0
block_cap = 1024

def phase_pair(kpart, coords):
    theta = kpart[0][:, None] * coords[0][None, :] + kpart[1][:, None] * coords[1][None, :] + kpart[2][:, None] * coords[2][None, :]
    return (jnp.cos(theta).astype(jnp.bfloat16), jnp.sin(theta).astype(jnp.bfloat16))

def reference(positions, features, counts, ghost_index, kvec, screen_len, long_weight, short_weight):
    devices = N_DOM * N_SLAB
    width = math.gcd(K_VEC, block_cap)
    nblocks = K_VEC // width
    kscaled = kvec.astype(jnp.float32) * (2.0 * math.pi / box_length)
    ksq = kscaled[0] * kscaled[0] + kscaled[1] * kscaled[1] + kscaled[2] * kscaled[2]
    slots = lax.iota(jnp.int32, ATOM_DEV)
    valid = (slots[None, :] < counts[:, None]).astype(jnp.float32)
    pos_blocks = positions.reshape(3, devices, ATOM_DEV).transpose(1, 0, 2)
    feat_blocks = features.reshape(C, devices, ATOM_DEV).transpose(1, 0, 2)
    masked = (feat_blocks.astype(jnp.float32) * valid[:, None, :]).astype(jnp.bfloat16)

    def factor_block(total, item):
        coords, values = item

        def one(index):
            kpart = lax.dynamic_slice_in_dim(kscaled, index * width, width, 1)
            cosine, sine = phase_pair(kpart, coords)
            real = lax.dot_general(cosine, values, (((1,), (1,)), ((), ())), preferred_element_type=jnp.float32)
            imag = lax.dot_general(sine, values, (((1,), (1,)), ((), ())), preferred_element_type=jnp.float32)
            return jnp.concatenate([real, imag], axis=1)
        term = lax.map(one, jnp.arange(nblocks, dtype=jnp.int32)).reshape(K_VEC, 2 * C)
        return (total + term, None)
    summed, unused = lax.scan(factor_block, jnp.zeros((K_VEC, 2 * C), jnp.float32), (pos_blocks, masked))
    filt = 1.0 / (1.0 + ksq[:, None] * (screen_len * screen_len)[None, :])
    filtered = (summed * jnp.concatenate([filt, filt], axis=1)).astype(jnp.bfloat16)
    export_all = jnp.concatenate([pos_blocks, masked.astype(jnp.float32)], axis=1)
    export = jax.vmap(lambda e, i: jnp.take(e, i, axis=1))(export_all, ghost_index)
    export = export.reshape(N_DOM, N_SLAB, 3 + C, 2 * GHOST)
    from_lower = jnp.roll(export, 1, axis=0)[..., GHOST:]
    from_upper = jnp.roll(export, -1, axis=0)[..., :GHOST]
    remote = jnp.concatenate([from_lower, from_upper], axis=-1).reshape(devices, 3 + C, 2 * GHOST)
    long_scale = long_gain / math.sqrt(K_VEC * ATOMS)
    long_mix = long_weight.astype(jnp.float32).T
    short_mix = short_weight.astype(jnp.float32).T

    def per_block(item):
        coords, values, live, ghosts, initial = item

        def step(index, acc):
            lo = index * width
            kpart = lax.dynamic_slice_in_dim(kscaled, lo, width, 1)
            cosine, sine = phase_pair(kpart, coords)
            rows = lax.dynamic_slice_in_dim(filtered, lo, width, 0)
            acc = acc + lax.dot_general(rows[:, :C], cosine, (((0,), (0,)), ((), ())), preferred_element_type=jnp.float32)
            return acc + lax.dot_general(rows[:, C:], sine, (((0,), (0,)), ((), ())), preferred_element_type=jnp.float32)
        longmsg = lax.fori_loop(0, nblocks, step, jnp.zeros((C, ATOM_DEV), jnp.float32))
        partner_pos = jnp.concatenate([coords, ghosts[:3]], axis=1)
        partner_feat = jnp.concatenate([values, ghosts[3:].astype(jnp.bfloat16)], axis=1)
        partner_live = jnp.concatenate([live, jnp.ones((2 * GHOST,), jnp.float32)])
        squares = []
        for dim in range(3):
            diff = coords[dim][:, None] - partner_pos[dim][None, :]
            diff = diff - box_length * jnp.floor(diff / box_length + 0.5)
            squares.append(diff * diff)
        radius = squares[0] + squares[1] + squares[2]
        pair = (jnp.exp(-radius / pair_scale) * partner_live[None, :]).astype(jnp.bfloat16)
        shortmsg = lax.dot_general(partner_feat, pair, (((1,), (1,)), ((), ())), preferred_element_type=jnp.float32)
        mixed = initial.astype(jnp.float32) + long_scale * jnp.dot(long_mix, longmsg, precision=lax.Precision.HIGHEST) + short_gain * jnp.dot(short_mix, shortmsg, precision=lax.Precision.HIGHEST)
        return (mixed * live[None, :]).astype(jnp.bfloat16)
    result = lax.map(per_block, (pos_blocks, masked, valid, remote, feat_blocks))
    return result.transpose(1, 0, 2).reshape(C, ATOMS)
```

```python
import math

import jax
import jax.numpy as jnp
import numpy as np
from jax import lax
from jax.experimental import pallas as pl
from jax.experimental.pallas import tpu as pltpu
from jax.sharding import Mesh, PartitionSpec as P

box_length = 216.0
pair_scale = 12.5
short_gain = 0.5
long_gain = 16.0
vmem_limit = 48 * 1024 * 1024

ALL = ("x", "zh", "core", "y", "zl")
DOM = ("x", "zh", "core")
NEAR = ("x", "core")
FAR = ("zh", "y", "zl")

f32 = jnp.float32
bf16 = jnp.bfloat16


def fit_cos(degree):
    nodes = np.cos(np.pi * (np.arange(64) + 0.5) / 64)
    w = 0.125 * (nodes + 1.0)
    cheb = np.polynomial.chebyshev.Chebyshev.fit(w, np.cos(2 * np.pi * np.sqrt(w)), degree, domain=[0.0, 0.25])
    return [float(c) for c in cheb.convert(kind=np.polynomial.Polynomial).coef]


COS_POLY = fit_cos(6)


def turn_cos(v):
    r = v - jnp.floor(v + 0.5)
    w = r * r
    acc = w * COS_POLY[-1] + COS_POLY[-2]
    for c in COS_POLY[-3::-1]:
        acc = acc * w + c
    return acc


def table(coord, kind):
    row = lax.broadcasted_iota(jnp.int32, (8 if kind == "y" else 24, 1), 0)
    if kind == "x":
        freq = 4 * (row >> 3) + (row & 3) + 1
        sine = (row & 4) != 0
    elif kind == "z":
        freq = 2 * (row >> 2) + (row & 1) + 1
        sine = (row & 2) != 0
    else:
        freq = jnp.where(row < 2, 5, jnp.where(row < 4, 10, jnp.where(row < 6, 1, 2)))
        sine = (row & 1) != 0
    return turn_cos(freq.astype(f32) * (coord * (1.0 / box_length)) - jnp.where(sine, 0.25, 0.0))


def first_rows(rows):
    sub = lax.broadcasted_iota(jnp.int32, rows.shape, 0)
    return jnp.where(sub < 4, rows, jnp.where(sub == 4, 1.0, 0.0))


def wide_rows(xtab, ytab):
    groups = []
    for g in range(3):
        groups += [xtab[8 * g : 8 * g + 8] * ytab[f : f + 1] for f in range(4)]
    groups += [xtab[8 * g : 8 * g + 8] for g in range(3)]
    return groups + [first_rows(ytab)]


def tall_rows(ztab, ytab):
    sub = lax.broadcasted_iota(jnp.int32, ytab.shape, 0)
    groups = []
    for b in range(2):
        wave = jnp.where(sub < 4, ytab[4 + 2 * b : 5 + 2 * b], ytab[5 + 2 * b : 6 + 2 * b])
        for h in range(6):
            four = ztab[4 * h : 4 * h + 4]
            groups.append(jnp.concatenate([four, four], axis=0) * wave)
    groups += [ztab[8 * g : 8 * g + 8] for g in range(3)]
    return groups + [first_rows(jnp.concatenate([ytab[4:8], ytab[0:4]], axis=0))]


def store_wide(xcoord, ytab, e_ref):
    groups = wide_rows(table(xcoord, "x"), ytab)
    for n in range(0, 16, 2):
        two = jnp.concatenate(groups[n : n + 2], axis=0)
        high = two.astype(bf16)
        e_ref[8 * n : 8 * n + 16, :] = high
        e_ref[128 + 8 * n : 128 + 8 * n + 16, :] = (two - high.astype(f32)).astype(bf16)


def wide_code(lane):
    group, low = lane >> 3, lane & 7
    p = jnp.where(group < 12, 4 * (group >> 2), 4 * (group - 12)) + (low & 3) + 1
    p = jnp.where(group < 15, p, 0)
    a = jnp.where(group < 12, 1 + ((group >> 1) & 1), 0)
    a = jnp.where((group == 15) & (low < 4), 1 + (low >> 1), a)
    return p, a, lane < 125


def wide_masks(lane):
    group, low = lane >> 3, lane & 7
    m_x = jnp.where(group < 15, 4, 0)
    m_a = jnp.where(group < 12, 8, jnp.where((group == 15) & (low < 4), 1, 0))
    s_x = jnp.where((low & 4) != 0, 1.0, -1.0)
    s_a = jnp.where(jnp.where(group < 12, group & 1, low & 1) != 0, 1.0, -1.0)
    return m_x, m_a, s_x, s_a


def tall_code(group, sub):
    mixed, plain = group < 12, group < 15
    r = jnp.where(mixed, 2 * (group % 6) + (sub & 1) + 1, 4 * (group - 12) + 2 * (sub >> 2) + (sub & 1) + 1)
    r = jnp.where(plain, r, 0)
    b = jnp.where(mixed, 1 + group // 6, jnp.where(plain, 0, jnp.where(sub < 4, 1 + (sub >> 1), 0)))
    return b, r, plain | (sub < 5)


def tall_masks(group, sub):
    mixed, plain = group < 12, group < 15
    m_b = jnp.where(mixed, 4, jnp.where(plain, 0, jnp.where(sub < 4, 1, 0)))
    m_z = jnp.where(plain, 2 + 0 * sub, 0)
    s_b = jnp.where(jnp.where(mixed, sub & 4, sub & 1) != 0, 1.0, -1.0)
    s_z = jnp.where((sub & 2) != 0, 1.0, -1.0)
    return m_b, m_z, s_b, s_z


def prep_kernel(count_ref, pos_ref, feat_ref, idx_ref, pay_ref, low_ref, high_ref):
    atoms = pos_ref.shape[1]
    ghost = idx_ref.shape[1] // 2
    slot = lax.broadcasted_iota(jnp.int32, (1, atoms), 1)
    valid = (slot < count_ref[0]).astype(f32)
    masked = feat_ref[...].astype(f32) * valid
    pos = pos_ref[...]
    tail = jnp.concatenate([pos, jnp.zeros((1, atoms), f32)], axis=0)
    for g in range(pay_ref.shape[0]):
        pay_ref[g] = jnp.concatenate([masked[4 * g : 4 * g + 4], tail], axis=0)
    hi = tail.astype(bf16)
    rest = tail - hi.astype(f32)
    mid = rest.astype(bf16)
    lo = (rest - mid.astype(f32)).astype(bf16)
    table = jnp.concatenate(
        [masked.astype(bf16).astype(f32), hi.astype(f32), mid.astype(f32), lo.astype(f32), jnp.zeros((4, atoms), f32)], axis=0
    ).astype(bf16)
    half = 2 * ghost
    row = lax.broadcasted_iota(jnp.int32, (half, ghost), 0)
    for n, out in ((0, low_ref), (1, high_ref)):
        want = idx_ref[0:1, n * ghost : (n + 1) * ghost] - n * half
        pick = (row == want).astype(f32).astype(bf16)
        got = jnp.dot(table[:, n * half : (n + 1) * half], pick, preferred_element_type=f32)
        out[0:32, :] = got[0:32]
        place = (got[32:36] + got[36:40]) + got[40:44]
        out[32:40, :] = jnp.concatenate([place, jnp.zeros((4, ghost), f32)], axis=0)


def factor_kernel(in_ref, out_ref, e_ref, m_ref, acc_ref):
    step = pl.program_id(0)
    ytab = table(in_ref[0, 5:6, :], "y")
    store_wide(in_ref[0, 4:5, :], ytab, e_ref)
    groups = tall_rows(table(in_ref[0, 6:7, :], "z"), ytab)
    for c in range(4):
        line = in_ref[0, c : c + 1, :]
        for n in range(0, 16, 2):
            at = 128 * c + 8 * n
            m_ref[at : at + 16, :] = jnp.concatenate([line * groups[n], line * groups[n + 1]], axis=0).astype(bf16)
    term = lax.dot_general(m_ref[...], e_ref[...], (((1,), (1,)), ((), ())), preferred_element_type=f32)

    @pl.when(step == 0)
    def _():
        acc_ref[...] = term

    @pl.when(step > 0)
    def _():
        acc_ref[...] += term

    @pl.when(step == pl.num_programs(0) - 1)
    def _():
        for n in range(out_ref.shape[0]):
            out_ref[n] = acc_ref[8 * n : 8 * n + 8, 0:128] + acc_ref[8 * n : 8 * n + 8, 128:256]


def coef_kernel(where_ref, kvec_ref, screen_ref, out_ref):
    owner = where_ref[0]
    group = owner % 16
    chan = 4 * where_ref[1] + owner // 16

    p_c, a_c, used_c = wide_code(lax.broadcasted_iota(jnp.int32, (128, 1), 0))
    code_c = jnp.where(used_c, 4 * p_c + a_c, -1)
    b_r, r_r, used_r = tall_code(group, lax.broadcasted_iota(jnp.int32, (8, 1), 0))
    code_r = jnp.where(used_r, 4 * r_r + b_r, -1)
    width = 1024
    counts = jnp.zeros((64, 128), f32)
    for n in range(kvec_ref.shape[1] // width):
        at = slice(n * width, (n + 1) * width)
        kx, ky, kz = kvec_ref[0:1, at], kvec_ref[1:2, at], kvec_ref[2:3, at]
        size = jnp.abs(ky)
        turn = jnp.where(ky < 0, -1, 1)
        ka = jnp.where(size >= 8, 2, jnp.where(size >= 3, 1, 0))
        kb = turn * (size - 5 * ka)
        wide = jnp.where(code_c == 4 * jnp.abs(kx) + ka, 1.0, 0.0).astype(bf16)
        hit = jnp.where(code_r == 4 * jnp.abs(kz) + jnp.abs(kb), 1.0, 0.0)
        sx, sa, sb, sz = (jnp.clip(k, -1, 1).astype(f32) for k in (kx, turn * ka, kb, kz))
        signs = [sx * sa, sx * sb, sx * sz, sa * sb, sa * sz, sb * sz, (sx * sa) * (sb * sz)]
        lines = jnp.concatenate([hit] + [hit * sign for sign in signs], axis=0).astype(bf16)
        counts = counts + lax.dot_general(lines, wide, (((1,), (1,)), ((), ())), preferred_element_type=f32)
    n_0, n_xa, n_xb, n_xz, n_ab, n_az, n_bz, n_all = (counts[8 * v : 8 * v + 8] for v in range(8))

    lane = lax.broadcasted_iota(jnp.int32, (8, 128), 1)
    sub = lax.broadcasted_iota(jnp.int32, (8, 128), 0)
    p, a, used_l = wide_code(lane)
    b, r, used_s = tall_code(group, sub)
    _, _, s_x, s_a = wide_masks(lane)
    _, _, s_b, s_z = tall_masks(group, sub)
    unit = 2.0 * math.pi / box_length
    screen = unit * screen_ref[pl.ds(chan, 1), :]
    screen = screen * screen

    def filt(q):
        return 1.0 / (1.0 + (p * p + q * q + r * r).astype(f32) * screen)

    like, unlike = filt(5 * a + b), filt(5 * a - b)
    used = used_l & used_s
    mean = jnp.where(used, 0.5 * (like + unlike), 0.0)
    half = jnp.where(used, 0.5 * (like - unlike), 0.0)
    out_ref[0] = mean * n_0 + half * n_ab
    out_ref[1] = -(s_x * s_a) * (mean * n_xa + half * n_xb)
    out_ref[2] = -(s_x * s_b) * (mean * n_xb + half * n_xa)
    out_ref[3] = -(s_x * s_z) * (mean * n_xz + half * n_all)
    out_ref[4] = -(s_a * s_b) * (mean * n_ab + half * n_0)
    out_ref[5] = -(s_a * s_z) * (mean * n_az + half * n_bz)
    out_ref[6] = -(s_b * s_z) * (mean * n_bz + half * n_az)
    out_ref[7] = (s_x * s_a) * (s_b * s_z) * (mean * n_all + half * n_xz)


def owner_kernel(where_ref, part_ref, coef_ref, out_ref):
    group = where_ref[0] % 16
    totals = [part_ref[n] for n in range(4)]
    for n in range(4, part_ref.shape[0]):
        totals[n % 4] = totals[n % 4] + part_ref[n]
    total = (totals[0] + totals[1]) + (totals[2] + totals[3])
    lane = lax.broadcasted_iota(jnp.int32, (8, 128), 1)
    sub = lax.broadcasted_iota(jnp.int32, (8, 128), 0)
    m_x, m_a, _, _ = wide_masks(lane)
    m_b, m_z, _, _ = tall_masks(group, sub)

    def lanes(value, mask):
        return jnp.take_along_axis(value, lane ^ mask, axis=1)

    def rows(value, mask):
        return jnp.take_along_axis(value, sub ^ mask, axis=0)

    t_x, t_a, t_xa = lanes(total, m_x), lanes(total, m_a), lanes(total, m_x ^ m_a)
    terms = [
        total,
        t_xa,
        rows(t_x, m_b),
        rows(t_x, m_z),
        rows(t_a, m_b),
        rows(t_a, m_z),
        rows(total, m_b ^ m_z),
        rows(t_xa, m_b ^ m_z),
    ]
    done = coef_ref[0] * terms[0]
    for n in range(1, 8):
        done = done + coef_ref[n] * terms[n]
    for n in range(out_ref.shape[0]):
        out_ref[n] = done


def field_kernel(filt_ref, in_ref, out_ref, e_ref, g_ref):
    step = pl.program_id(0)

    @pl.when(step == 0)
    def _():
        for n in range(0, filt_ref.shape[0], 2):
            two = jnp.concatenate([filt_ref[n], filt_ref[n + 1]], axis=0).astype(bf16)
            g_ref[8 * n : 8 * n + 16, 0:128] = two
            g_ref[8 * n : 8 * n + 16, 128:256] = two

    ytab = table(in_ref[0, 5:6, :], "y")
    store_wide(in_ref[0, 4:5, :], ytab, e_ref)
    groups = tall_rows(table(in_ref[0, 6:7, :], "z"), ytab)
    term = jnp.dot(g_ref[...], e_ref[...], preferred_element_type=f32)
    lines = []
    for c in range(4):
        acc = term[128 * c : 128 * c + 8] * groups[0]
        for n in range(1, 16):
            acc = acc + term[128 * c + 8 * n : 128 * c + 8 * n + 8] * groups[n]
        lines.append(jnp.sum(acc, axis=0, keepdims=True))
    out_ref[0] = jnp.concatenate(lines, axis=0)


def valid_row(count_ref, atoms):
    slot = lax.broadcasted_iota(jnp.int32, (1, atoms), 1)
    return (slot < count_ref[0]).astype(f32)


def short_kernel(count_ref, pos_ref, feat_ref, g1_ref, g2_ref, out_ref):
    atoms = pos_ref.shape[1]
    masked = (feat_ref[...].astype(f32) * valid_row(count_ref, atoms)).astype(bf16)
    shrink = math.sqrt(math.log2(math.e) / pair_scale)
    box = box_length * shrink
    pos = pos_ref[...] * shrink
    xr, yr, zr = pos[0:1], pos[1:2], pos[2:3]
    pos8 = jnp.concatenate([pos, jnp.zeros((5, atoms), f32)], axis=0)

    def pairs(cols, wrap):
        dx = cols[:, 0:1] - xr
        if wrap:
            dx = jnp.abs(dx)
            dx = jnp.minimum(dx, box - dx)
        dy = cols[:, 1:2] - yr
        dz = jnp.abs(cols[:, 2:3] - zr)
        dz = jnp.minimum(dz, box - dz)
        return jnp.exp2(-(dx * dx + dy * dy + dz * dz)).astype(bf16)

    ghost = jnp.concatenate([g1_ref[...], g2_ref[...]], axis=1)
    cols = jnp.transpose(ghost[32:40] * shrink)
    short = jnp.dot(ghost[0:32].astype(bf16), pairs(cols, True), preferred_element_type=f32)
    step = 256
    for n in range(atoms // step):
        at = slice(n * step, (n + 1) * step)
        short = short + jnp.dot(masked[:, at], pairs(jnp.transpose(pos8[:, at]), False), preferred_element_type=f32)
    out_ref[...] = short


def final_kernel(count_ref, feat_ref, long_ref, short_ref, lw_ref, sw_ref, out_ref, *, long_scale):
    def mix(weight, value):
        hi = value.astype(bf16)
        lo = (value - hi.astype(f32)).astype(bf16)
        dims = (((0,), (0,)), ((), ()))
        return lax.dot_general(weight, hi, dims, preferred_element_type=f32) + lax.dot_general(
            weight, lo, dims, preferred_element_type=f32
        )

    feat = feat_ref[...].astype(f32)
    total = feat + long_scale * mix(lw_ref[...], long_ref[...]) + short_gain * mix(sw_ref[...], short_ref[...])
    out_ref[...] = (total * valid_row(count_ref, feat.shape[1])).astype(bf16)


def whole(memory=pltpu.VMEM):
    return pl.BlockSpec(memory_space=memory)


def local(positions, features, counts, ghost_index, kvec, screen_len, long_weight, short_weight):
    chans, atoms = features.shape
    total_vec = kvec.shape[1]
    ghost = ghost_index.shape[1] // 2
    near = lax.axis_size(NEAR)
    far = lax.axis_size(FAR)
    params = pltpu.CompilerParams(vmem_limit_bytes=vmem_limit)

    payload, low, high = pl.pallas_call(
        prep_kernel,
        name="prep",
        out_shape=[
            jax.ShapeDtypeStruct((near, 8, atoms), f32),
            jax.ShapeDtypeStruct((40, ghost), f32),
            jax.ShapeDtypeStruct((40, ghost), f32),
        ],
        in_specs=[whole(pltpu.SMEM), whole(), whole(), whole()],
        out_specs=[whole(), whole(), whole()],
        compiler_params=params,
    )(counts, positions, features, ghost_index)

    gathered = lax.all_to_all(payload, NEAR, 0, 0, tiled=True)
    partial = pl.pallas_call(
        factor_kernel,
        name="factor",
        grid=(near,),
        out_shape=jax.ShapeDtypeStruct((far, 8, 128), f32),
        in_specs=[pl.BlockSpec((1, 8, atoms), lambda b: (b, 0, 0))],
        out_specs=pl.BlockSpec((far, 8, 128), lambda b: (0, 0, 0)),
        scratch_shapes=[pltpu.VMEM((256, atoms), bf16), pltpu.VMEM((512, atoms), bf16), pltpu.VMEM((512, 256), f32)],
        compiler_params=params,
    )(gathered)
    place = jnp.stack([lax.axis_index(FAR), lax.axis_index(NEAR)]).astype(jnp.int32)
    screens = jnp.broadcast_to(screen_len[:, None], (chans, 128))
    partial, low, high, kvec = lax.optimization_barrier((partial, low, high, kvec))
    spread = lax.all_to_all(partial, FAR, 0, 0, tiled=True)
    core = lax.axis_index("core")
    n_dom = lax.axis_size(DOM)
    flip = [(d, d ^ 1) for d in range(n_dom)]
    step = [(d, (d + 1) % n_dom if d % 2 else (d - 1) % n_dom) for d in range(n_dom)]
    ghosts_1 = lax.ppermute(jnp.where(core == 0, high, low), DOM, flip)
    ghosts_2 = lax.ppermute(jnp.where(core == 0, low, high), DOM, step)

    coef = pl.pallas_call(
        coef_kernel,
        name="coef",
        out_shape=jax.ShapeDtypeStruct((8, 8, 128), f32),
        in_specs=[whole(pltpu.SMEM), whole(), whole()],
        out_specs=whole(),
        compiler_params=params,
        cost_estimate=pl.CostEstimate(flops=2 * 64 * 256 * total_vec, bytes_accessed=8 * total_vec, transcendentals=0),
    )(place, kvec, screens)
    short = pl.pallas_call(
        short_kernel,
        name="short",
        out_shape=jax.ShapeDtypeStruct((chans, atoms), f32),
        in_specs=[whole(pltpu.SMEM)] + [whole()] * 4,
        out_specs=whole(),
        compiler_params=params,
        cost_estimate=pl.CostEstimate(flops=2 * 256 * 1280 * atoms, bytes_accessed=10 * 32 * atoms, transcendentals=1280 * atoms),
    )(counts, positions, features, ghosts_1, ghosts_2)
    spread, coef, short = lax.optimization_barrier((spread, coef, short))
    filtered = pl.pallas_call(
        owner_kernel,
        name="owner",
        out_shape=jax.ShapeDtypeStruct((far, 8, 128), f32),
        in_specs=[whole(pltpu.SMEM), whole(), whole()],
        out_specs=whole(),
        compiler_params=params,
    )(place, spread, coef)
    everywhere = lax.all_to_all(filtered, FAR, 0, 0, tiled=True)
    field = pl.pallas_call(
        field_kernel,
        name="field",
        grid=(near,),
        out_shape=jax.ShapeDtypeStruct((near, 4, atoms), f32),
        in_specs=[
            pl.BlockSpec((far, 8, 128), lambda b: (0, 0, 0)),
            pl.BlockSpec((1, 8, atoms), lambda b: (b, 0, 0)),
        ],
        out_specs=pl.BlockSpec((1, 4, atoms), lambda b: (b, 0, 0)),
        scratch_shapes=[pltpu.VMEM((256, atoms), bf16), pltpu.VMEM((512, 256), bf16)],
        compiler_params=params,
    )(everywhere, gathered)
    longmsg = lax.all_to_all(field, NEAR, 0, 0, tiled=True).reshape(chans, atoms)
    all_atoms = atoms * lax.axis_size(ALL)
    long_scale = long_gain / math.sqrt(total_vec * all_atoms)
    return pl.pallas_call(
        lambda *refs: final_kernel(*refs, long_scale=long_scale),
        name="final",
        out_shape=jax.ShapeDtypeStruct((chans, atoms), bf16),
        in_specs=[whole(pltpu.SMEM)] + [whole()] * 5,
        out_specs=whole(),
        compiler_params=params,
    )(counts, features, longmsg, short, long_weight, short_weight)


def solution(mesh):
    fine = Mesh(mesh.devices.reshape(4, 2, 2, 8, 4), ALL)
    return jax.shard_map(
        local,
        mesh=fine,
        in_specs=(P(None, ALL), P(None, ALL), P(ALL), P(ALL, None), P(), P(), P(), P()),
        out_specs=P(None, ALL),
        check_vma=False,
    )
```

```python
import math

import jax
import jax.numpy as jnp
import numpy as np
from jax import lax
from jax.experimental import pallas as pl
from jax.experimental.pallas import tpu as pltpu
from jax.sharding import Mesh, PartitionSpec as P

box_length = 216.0
pair_scale = 12.5
short_gain = 0.5
long_gain = 16.0
vmem_limit = 48 * 1024 * 1024

ALL = ("x", "zh", "core", "y", "zl")
DOM = ("x", "zh", "core")
NEAR = ("x", "core")
FAR = ("zh", "y", "zl")

f32 = jnp.float32
bf16 = jnp.bfloat16


def fit_cos(degree):
    nodes = np.cos(np.pi * (np.arange(64) + 0.5) / 64)
    w = 0.125 * (nodes + 1.0)
    cheb = np.polynomial.chebyshev.Chebyshev.fit(w, np.cos(2 * np.pi * np.sqrt(w)), degree, domain=[0.0, 0.25])
    return [float(c) for c in cheb.convert(kind=np.polynomial.Polynomial).coef]


COS_POLY = fit_cos(6)


def turn_cos(v):
    r = v - jnp.floor(v + 0.5)
    w = r * r
    acc = w * COS_POLY[-1] + COS_POLY[-2]
    for c in COS_POLY[-3::-1]:
        acc = acc * w + c
    return acc


def table(coord, kind):
    row = lax.broadcasted_iota(jnp.int32, (8 if kind == "y" else 24, 1), 0)
    if kind == "x":
        freq = 4 * (row >> 3) + (row & 3) + 1
        sine = (row & 4) != 0
    elif kind == "z":
        freq = 2 * (row >> 2) + (row & 1) + 1
        sine = (row & 2) != 0
    else:
        freq = jnp.where(row < 2, 5, jnp.where(row < 4, 10, jnp.where(row < 6, 1, 2)))
        sine = (row & 1) != 0
    return turn_cos(freq.astype(f32) * (coord * (1.0 / box_length)) - jnp.where(sine, 0.25, 0.0))


def first_rows(rows):
    sub = lax.broadcasted_iota(jnp.int32, rows.shape, 0)
    return jnp.where(sub < 4, rows, jnp.where(sub == 4, 1.0, 0.0))


def wide_rows(xtab, ytab):
    groups = []
    for g in range(3):
        groups += [xtab[8 * g : 8 * g + 8] * ytab[f : f + 1] for f in range(4)]
    groups += [xtab[8 * g : 8 * g + 8] for g in range(3)]
    return groups + [first_rows(ytab)]


def tall_rows(ztab, ytab):
    sub = lax.broadcasted_iota(jnp.int32, ytab.shape, 0)
    groups = []
    for b in range(2):
        wave = jnp.where(sub < 4, ytab[4 + 2 * b : 5 + 2 * b], ytab[5 + 2 * b : 6 + 2 * b])
        for h in range(6):
            four = ztab[4 * h : 4 * h + 4]
            groups.append(jnp.concatenate([four, four], axis=0) * wave)
    groups += [ztab[8 * g : 8 * g + 8] for g in range(3)]
    return groups + [first_rows(jnp.concatenate([ytab[4:8], ytab[0:4]], axis=0))]


def store_wide(xcoord, ytab, e_ref, at):
    groups = wide_rows(table(xcoord, "x"), ytab)
    for n in range(0, 16, 2):
        two = jnp.concatenate(groups[n : n + 2], axis=0)
        high = two.astype(bf16)
        e_ref[8 * n : 8 * n + 16, at] = high
        e_ref[128 + 8 * n : 128 + 8 * n + 16, at] = (two - high.astype(f32)).astype(bf16)


def wide_code(lane):
    group, low = lane >> 3, lane & 7
    p = jnp.where(group < 12, 4 * (group >> 2), 4 * (group - 12)) + (low & 3) + 1
    p = jnp.where(group < 15, p, 0)
    a = jnp.where(group < 12, 1 + ((group >> 1) & 1), 0)
    a = jnp.where((group == 15) & (low < 4), 1 + (low >> 1), a)
    return p, a, lane < 125


def wide_masks(lane):
    group, low = lane >> 3, lane & 7
    m_x = jnp.where(group < 15, 4, 0)
    m_a = jnp.where(group < 12, 8, jnp.where((group == 15) & (low < 4), 1, 0))
    s_x = jnp.where((low & 4) != 0, 1.0, -1.0)
    s_a = jnp.where(jnp.where(group < 12, group & 1, low & 1) != 0, 1.0, -1.0)
    return m_x, m_a, s_x, s_a


def tall_code(group, sub):
    mixed, plain = group < 12, group < 15
    r = jnp.where(mixed, 2 * (group % 6) + (sub & 1) + 1, 4 * (group - 12) + 2 * (sub >> 2) + (sub & 1) + 1)
    r = jnp.where(plain, r, 0)
    b = jnp.where(mixed, 1 + group // 6, jnp.where(plain, 0, jnp.where(sub < 4, 1 + (sub >> 1), 0)))
    return b, r, plain | (sub < 5)


def tall_masks(group, sub):
    mixed, plain = group < 12, group < 15
    m_b = jnp.where(mixed, 4, jnp.where(plain, 0, jnp.where(sub < 4, 1, 0)))
    m_z = jnp.where(plain, 2 + 0 * sub, 0)
    s_b = jnp.where(jnp.where(mixed, sub & 4, sub & 1) != 0, 1.0, -1.0)
    s_z = jnp.where((sub & 2) != 0, 1.0, -1.0)
    return m_b, m_z, s_b, s_z


def valid_row(count_ref, atoms):
    slot = lax.broadcasted_iota(jnp.int32, (1, atoms), 1)
    return (slot < count_ref[0]).astype(f32)


def prep_kernel(count_ref, pos_hbm, feat_hbm, pay_ref, pos_ref, feat_ref, sems):
    copies = [
        pltpu.make_async_copy(feat_hbm, feat_ref, sems.at[0]),
        pltpu.make_async_copy(pos_hbm, pos_ref, sems.at[1]),
    ]
    for copy in copies:
        copy.start()
    for copy in copies:
        copy.wait()
    atoms = pos_ref.shape[1]
    masked = feat_ref[...].astype(f32) * valid_row(count_ref, atoms)
    tail = jnp.concatenate([pos_ref[...], jnp.zeros((1, atoms), f32)], axis=0)
    for g in range(pay_ref.shape[0]):
        pay_ref[g] = jnp.concatenate([masked[4 * g : 4 * g + 4], tail], axis=0)


def faces_kernel(count_ref, core_ref, pos_ref, feat_ref, idx_ref, after_ref, flip_ref, step_ref):
    del after_ref
    atoms = pos_ref.shape[1]
    ghost = idx_ref.shape[1] // 2
    masked = feat_ref[...].astype(f32) * valid_row(count_ref, atoms)
    tail = jnp.concatenate([pos_ref[...], jnp.zeros((1, atoms), f32)], axis=0)
    hi = tail.astype(bf16).astype(f32)
    mid = (tail - hi).astype(bf16).astype(f32)
    lo = (tail - hi) - mid
    parts = jnp.concatenate([masked, hi, mid, lo, jnp.zeros((4, atoms), f32)], axis=0).astype(bf16)
    half = 2 * ghost
    row = lax.broadcasted_iota(jnp.int32, (half, ghost), 0)
    faces = []
    for n in range(2):
        want = idx_ref[0:1, n * ghost : (n + 1) * ghost] - n * half
        pick = (row == want).astype(f32).astype(bf16)
        got = jnp.dot(parts[:, n * half : (n + 1) * half], pick, preferred_element_type=f32)
        place = (got[32:36] + got[36:40]) + got[40:44]
        faces.append(jnp.concatenate([got[0:32], place, jnp.zeros((4, ghost), f32)], axis=0))
    first = core_ref[0] == 0
    flip_ref[...] = jnp.where(first, faces[1], faces[0])
    step_ref[...] = jnp.where(first, faces[0], faces[1])


def factor_kernel(in_ref, out_ref, e_ref, m_ref):
    blocks, _, atoms = in_ref.shape
    total = None
    for k in range(blocks):
        cols = slice(k * atoms, (k + 1) * atoms)
        ytab = table(in_ref[k, 5:6, :], "y")
        store_wide(in_ref[k, 4:5, :], ytab, e_ref, cols)
        groups = tall_rows(table(in_ref[k, 6:7, :], "z"), ytab)
        for c in range(4):
            line = in_ref[k, c : c + 1, :]
            for n in range(0, 16, 2):
                at = 128 * c + 8 * n
                m_ref[at : at + 16, cols] = jnp.concatenate([line * groups[n], line * groups[n + 1]], axis=0).astype(bf16)
        if k % 2:
            cols = slice((k - 1) * atoms, (k + 1) * atoms)
            dims = (((1,), (1,)), ((), ()))
            term = lax.dot_general(m_ref[:, cols], e_ref[:, cols], dims, preferred_element_type=f32)
            total = term if total is None else total + term
    out_ref[...] = (total[:, 0:128] + total[:, 128:256]).astype(bf16)


def coef_kernel(where_ref, kvec_ref, screen_ref, after_ref, out_ref):
    del after_ref
    owner = where_ref[0]
    group = owner % 16
    chan = 4 * where_ref[1] + owner // 16

    p_c, a_c, used_c = wide_code(lax.broadcasted_iota(jnp.int32, (128, 1), 0))
    code_c = jnp.where(used_c, 4 * p_c + a_c, -1)
    b_r, r_r, used_r = tall_code(group, lax.broadcasted_iota(jnp.int32, (8, 1), 0))
    code_r = jnp.where(used_r, 4 * r_r + b_r, -1)
    width = 1024
    counts = jnp.zeros((64, 128), f32)
    for n in range(kvec_ref.shape[1] // width):
        at = slice(n * width, (n + 1) * width)
        kx, ky, kz = kvec_ref[0:1, at], kvec_ref[1:2, at], kvec_ref[2:3, at]
        size = jnp.abs(ky)
        turn = jnp.where(ky < 0, -1, 1)
        ka = jnp.where(size >= 8, 2, jnp.where(size >= 3, 1, 0))
        kb = turn * (size - 5 * ka)
        wide = jnp.where(code_c == 4 * jnp.abs(kx) + ka, 1.0, 0.0).astype(bf16)
        hit = jnp.where(code_r == 4 * jnp.abs(kz) + jnp.abs(kb), 1.0, 0.0)
        sx, sa, sb, sz = (jnp.clip(k, -1, 1).astype(f32) for k in (kx, turn * ka, kb, kz))
        signs = [sx * sa, sx * sb, sx * sz, sa * sb, sa * sz, sb * sz, (sx * sa) * (sb * sz)]
        lines = jnp.concatenate([hit] + [hit * sign for sign in signs], axis=0).astype(bf16)
        counts = counts + lax.dot_general(lines, wide, (((1,), (1,)), ((), ())), preferred_element_type=f32)
    n_0, n_xa, n_xb, n_xz, n_ab, n_az, n_bz, n_all = (counts[8 * v : 8 * v + 8] for v in range(8))

    lane = lax.broadcasted_iota(jnp.int32, (8, 128), 1)
    sub = lax.broadcasted_iota(jnp.int32, (8, 128), 0)
    p, a, used_l = wide_code(lane)
    b, r, used_s = tall_code(group, sub)
    _, _, s_x, s_a = wide_masks(lane)
    _, _, s_b, s_z = tall_masks(group, sub)
    unit = 2.0 * math.pi / box_length
    screen = unit * screen_ref[pl.ds(chan, 1), :]
    screen = screen * screen

    def filt(q):
        return 1.0 / (1.0 + (p * p + q * q + r * r).astype(f32) * screen)

    like, unlike = filt(5 * a + b), filt(5 * a - b)
    used = used_l & used_s
    mean = jnp.where(used, 0.5 * (like + unlike), 0.0)
    half = jnp.where(used, 0.5 * (like - unlike), 0.0)
    out_ref[0] = mean * n_0 + half * n_ab
    out_ref[1] = -(s_x * s_a) * (mean * n_xa + half * n_xb)
    out_ref[2] = -(s_x * s_b) * (mean * n_xb + half * n_xa)
    out_ref[3] = -(s_x * s_z) * (mean * n_xz + half * n_all)
    out_ref[4] = -(s_a * s_b) * (mean * n_ab + half * n_0)
    out_ref[5] = -(s_a * s_z) * (mean * n_az + half * n_bz)
    out_ref[6] = -(s_b * s_z) * (mean * n_bz + half * n_az)
    out_ref[7] = (s_x * s_a) * (s_b * s_z) * (mean * n_all + half * n_xz)


def owner_kernel(where_ref, part_ref, coef_ref, step_ref, g1_ref, out_ref, step_out):
    del g1_ref
    step_out[...] = step_ref[...]
    group = where_ref[0] % 16
    totals = [part_ref[16 * n : 16 * n + 16, :].astype(f32) for n in range(4)]
    for n in range(4, part_ref.shape[0] // 16):
        totals[n % 4] = totals[n % 4] + part_ref[16 * n : 16 * n + 16, :].astype(f32)
    total = (totals[0] + totals[1]) + (totals[2] + totals[3])
    total = total[0:8] + total[8:16]
    lane = lax.broadcasted_iota(jnp.int32, (8, 128), 1)
    sub = lax.broadcasted_iota(jnp.int32, (8, 128), 0)
    m_x, m_a, _, _ = wide_masks(lane)
    m_b, m_z, _, _ = tall_masks(group, sub)

    def lanes(value, mask):
        return jnp.take_along_axis(value, lane ^ mask, axis=1)

    def rows(value, mask):
        return jnp.take_along_axis(value, sub ^ mask, axis=0)

    t_x, t_a, t_xa = lanes(total, m_x), lanes(total, m_a), lanes(total, m_x ^ m_a)
    terms = [
        total,
        t_xa,
        rows(t_x, m_b),
        rows(t_x, m_z),
        rows(t_a, m_b),
        rows(t_a, m_z),
        rows(total, m_b ^ m_z),
        rows(t_xa, m_b ^ m_z),
    ]
    done = coef_ref[0] * terms[0]
    for n in range(1, 8):
        done = done + coef_ref[n] * terms[n]
    twice = jnp.concatenate([done, done], axis=0).astype(bf16)
    for n in range(out_ref.shape[0] // 16):
        out_ref[16 * n : 16 * n + 16, :] = twice


def field_kernel(filt_ref, in_ref, g2_ref, out_ref, e_ref, g_ref):
    del g2_ref
    g_ref[:, 0:128] = filt_ref[...]
    g_ref[:, 128:256] = filt_ref[...]
    blocks, _, atoms = out_ref.shape
    for k in range(blocks):
        cols = slice(k * atoms, (k + 1) * atoms)
        ytab = table(in_ref[k, 5:6, :], "y")
        store_wide(in_ref[k, 4:5, :], ytab, e_ref, cols)
        groups = tall_rows(table(in_ref[k, 6:7, :], "z"), ytab)
        term = jnp.dot(g_ref[...], e_ref[:, cols], preferred_element_type=f32)
        lines = []
        for c in range(4):
            acc = term[128 * c : 128 * c + 8] * groups[0]
            for n in range(1, 16):
                acc = acc + term[128 * c + 8 * n : 128 * c + 8 * n + 8] * groups[n]
            lines.append(jnp.sum(acc, axis=0, keepdims=True))
        out_ref[k] = jnp.concatenate(lines, axis=0)


shrink = math.sqrt(math.log2(math.e) / pair_scale)


def pairs(cols, rows, wrap):
    box = box_length * shrink
    dx = cols[:, 0:1] - rows[0:1]
    if wrap:
        dx = jnp.abs(dx)
        dx = jnp.minimum(dx, box - dx)
    dy = cols[:, 1:2] - rows[1:2]
    dz = jnp.abs(cols[:, 2:3] - rows[2:3])
    dz = jnp.minimum(dz, box - dz)
    return jnp.exp2(-(dx * dx + dy * dy + dz * dz)).astype(bf16)


def short_kernel(
    count_ref, pos_ref, feat_ref, g1_ref, g2_ref, lw_ref, sw_ref, after_ref, base_ref, twice_ref
):
    del after_ref
    atoms = pos_ref.shape[1]
    feat = feat_ref[...].astype(f32)
    masked = (feat * valid_row(count_ref, atoms)).astype(bf16)
    rows = pos_ref[...] * shrink
    rows8 = jnp.concatenate([rows, jnp.zeros((5, atoms), f32)], axis=0)
    ghost = jnp.concatenate([g1_ref[...], g2_ref[...]], axis=1)
    near_by = pairs(jnp.transpose(ghost[32:40] * shrink), rows, True)
    short = jnp.dot(ghost[0:32].astype(bf16), near_by, preferred_element_type=f32)
    step = 256
    for n in range(atoms // step):
        at = slice(n * step, (n + 1) * step)
        own = pairs(jnp.transpose(rows8[:, at]), rows, False)
        short = short + jnp.dot(masked[:, at], own, preferred_element_type=f32)
    mixed = jnp.dot(stacked(sw_ref[...]), split(short), preferred_element_type=f32)
    base_ref[...] = feat + short_gain * mixed
    twice_ref[...] = stacked(lw_ref[...])


def stacked(weight):
    turned = jnp.transpose(weight.astype(f32))
    return jnp.concatenate([turned, turned], axis=1).astype(bf16)


def split(value):
    high = value.astype(bf16)
    low = (value - high.astype(f32)).astype(bf16)
    return jnp.concatenate([high, low], axis=0)


def final_kernel(count_ref, base_ref, long_ref, twice_ref, out_ref, *, long_scale):
    mixed = jnp.dot(twice_ref[...], split(long_ref[...]), preferred_element_type=f32)
    total = base_ref[...] + long_scale * mixed
    out_ref[...] = (total * valid_row(count_ref, total.shape[1])).astype(bf16)


def whole(memory=pltpu.VMEM):
    return pl.BlockSpec(memory_space=memory)


def local(positions, features, counts, ghost_index, kvec, screen_len, long_weight, short_weight):
    chans, atoms = features.shape
    total_vec = kvec.shape[1]
    ghost = ghost_index.shape[1] // 2
    near = lax.axis_size(NEAR)
    far = lax.axis_size(FAR)
    params = pltpu.CompilerParams(vmem_limit_bytes=vmem_limit)

    payload = pl.pallas_call(
        prep_kernel,
        name="prep",
        out_shape=jax.ShapeDtypeStruct((near, 8, atoms), f32),
        in_specs=[whole(pltpu.SMEM), whole(pl.ANY), whole(pl.ANY)],
        out_specs=whole(),
        scratch_shapes=[
            pltpu.VMEM(positions.shape, f32),
            pltpu.VMEM(features.shape, bf16),
            pltpu.SemaphoreType.DMA((2,)),
        ],
    )(counts, positions, features)
    gathered = lax.all_to_all(payload, NEAR, 0, 0, tiled=True)

    rows = jax.ShapeDtypeStruct((8 * far, 128), bf16)

    def exchange(value):
        return lax.all_to_all(value.reshape(far, 8, 128), FAR, 0, 0, tiled=True).reshape(8 * far, 128)

    partial = pl.pallas_call(
        factor_kernel,
        name="factor",
        out_shape=rows,
        in_specs=[whole()],
        out_specs=whole(),
        scratch_shapes=[pltpu.VMEM((256, near * atoms), bf16), pltpu.VMEM((512, near * atoms), bf16)],
        compiler_params=params,
    )(gathered)
    spread = exchange(partial)

    place = jnp.stack([lax.axis_index(FAR), lax.axis_index(NEAR)]).astype(jnp.int32)
    screens = jnp.broadcast_to(screen_len[:, None], (chans, 128))
    coef = pl.pallas_call(
        coef_kernel,
        name="coef",
        out_shape=jax.ShapeDtypeStruct((8, 8, 128), f32),
        in_specs=[whole(pltpu.SMEM), whole(), whole(), whole(pl.ANY)],
        out_specs=whole(),
        compiler_params=params,
        cost_estimate=pl.CostEstimate(flops=2 * 64 * 256 * total_vec, bytes_accessed=8 * total_vec, transcendentals=0),
    )(place, kvec, screens, partial)
    core = lax.axis_index("core").reshape(1).astype(jnp.int32)
    face = jax.ShapeDtypeStruct((chans + 8, ghost), f32)
    flip_face, step_face = pl.pallas_call(
        faces_kernel,
        name="faces",
        out_shape=[face, face],
        in_specs=[whole(pltpu.SMEM), whole(pltpu.SMEM), whole(), whole(), whole(), whole(pl.ANY)],
        out_specs=[whole(), whole()],
        compiler_params=params,
    )(counts, core, positions, features, ghost_index, partial)
    n_dom = lax.axis_size(DOM)
    flip = [(d, d ^ 1) for d in range(n_dom)]
    step = [(d, (d + 1) % n_dom if d % 2 else (d - 1) % n_dom) for d in range(n_dom)]
    ghosts_1 = lax.ppermute(flip_face, DOM, flip)
    filtered, step_face = pl.pallas_call(
        owner_kernel,
        name="owner",
        out_shape=[rows, face],
        in_specs=[whole(pltpu.SMEM)] + [whole()] * 3 + [whole(pl.ANY)],
        out_specs=[whole()] * 2,
        compiler_params=params,
    )(place, spread, coef, step_face, ghosts_1)
    everywhere = exchange(filtered)
    ghosts_2 = lax.ppermute(step_face, DOM, step)
    field = pl.pallas_call(
        field_kernel,
        name="field",
        out_shape=jax.ShapeDtypeStruct((near, 4, atoms), f32),
        in_specs=[whole(), whole(), whole(pl.ANY)],
        out_specs=whole(),
        scratch_shapes=[pltpu.VMEM((256, near * atoms), bf16), pltpu.VMEM((512, 256), bf16)],
        compiler_params=params,
    )(everywhere, gathered, ghosts_2)
    base, twice = pl.pallas_call(
        short_kernel,
        name="short",
        out_shape=[jax.ShapeDtypeStruct((chans, atoms), f32), jax.ShapeDtypeStruct((chans, 2 * chans), bf16)],
        in_specs=[whole(pltpu.SMEM)] + [whole()] * 6 + [whole(pl.ANY)],
        out_specs=[whole()] * 2,
        compiler_params=params,
        cost_estimate=pl.CostEstimate(flops=2 * 256 * 1280 * atoms, bytes_accessed=10 * 32 * atoms, transcendentals=1280 * atoms),
    )(counts, positions, features, ghosts_1, ghosts_2, long_weight, short_weight, field)
    longmsg = lax.all_to_all(field, NEAR, 0, 0, tiled=True).reshape(chans, atoms)
    all_atoms = atoms * lax.axis_size(ALL)
    long_scale = long_gain / math.sqrt(total_vec * all_atoms)
    return pl.pallas_call(
        lambda *refs: final_kernel(*refs, long_scale=long_scale),
        name="final",
        out_shape=jax.ShapeDtypeStruct((chans, atoms), bf16),
        in_specs=[whole(pltpu.SMEM)] + [whole()] * 3,
        out_specs=whole(),
        compiler_params=params,
    )(counts, base, longmsg, twice)


def solution(mesh):
    fine = Mesh(mesh.devices.reshape(4, 2, 2, 8, 4), ALL)
    return jax.shard_map(
        local,
        mesh=fine,
        in_specs=(P(None, ALL), P(None, ALL), P(ALL), P(ALL, None), P(), P(), P(), P()),
        out_specs=P(None, ALL),
        check_vma=False,
    )
```

```python
import math

import jax
import jax.numpy as jnp
import numpy as np
from jax import lax
from jax.experimental import pallas as pl
from jax.experimental.pallas import tpu as pltpu
from jax.sharding import Mesh, PartitionSpec as P

box_length = 216.0
pair_scale = 12.5
short_gain = 0.5
long_gain = 16.0
feature_top = 6.0
feature_steps = 32767.0
first_in = 59
first_out = 59
first_near = 4
vmem_limit = 48 * 1024 * 1024

ALL = ("x", "zh", "core", "y", "zl")
DOM = ("x", "zh", "core")
NEAR = ("x", "core")
FAR = ("zh", "y", "zl")

f32 = jnp.float32
bf16 = jnp.bfloat16


def fit_cos(degree):
    nodes = np.cos(np.pi * (np.arange(64) + 0.5) / 64)
    w = 0.125 * (nodes + 1.0)
    cheb = np.polynomial.chebyshev.Chebyshev.fit(w, np.cos(2 * np.pi * np.sqrt(w)), degree, domain=[0.0, 0.25])
    return [float(c) for c in cheb.convert(kind=np.polynomial.Polynomial).coef]


COS_POLY = fit_cos(6)


def turn_cos(v):
    r = v - jnp.floor(v + 0.5)
    w = r * r
    acc = w * COS_POLY[-1] + COS_POLY[-2]
    for c in COS_POLY[-3::-1]:
        acc = acc * w + c
    return acc


def table(turns, kind):
    row = lax.broadcasted_iota(jnp.int32, (8 if kind == "y" else 24, 1), 0)
    if kind == "x":
        freq = 4 * (row >> 3) + (row & 3) + 1
        sine = (row & 4) != 0
    elif kind == "z":
        freq = 2 * (row >> 2) + (row & 1) + 1
        sine = (row & 2) != 0
    else:
        freq = jnp.where(row < 2, 5, jnp.where(row < 4, 10, jnp.where(row < 6, 1, 2)))
        sine = (row & 1) != 0
    return turn_cos(freq.astype(f32) * turns - jnp.where(sine, 0.25, 0.0))


def first_rows(rows):
    sub = lax.broadcasted_iota(jnp.int32, rows.shape, 0)
    return jnp.where(sub < 4, rows, jnp.where(sub == 4, 1.0, 0.0))


def wide_rows(xtab, ytab):
    groups = []
    for g in range(3):
        groups += [xtab[8 * g : 8 * g + 8] * ytab[f : f + 1] for f in range(4)]
    groups += [xtab[8 * g : 8 * g + 8] for g in range(3)]
    return groups + [first_rows(ytab)]


def tall_rows(ztab, ytab):
    sub = lax.broadcasted_iota(jnp.int32, ytab.shape, 0)
    groups = []
    for b in range(2):
        wave = jnp.where(sub < 4, ytab[4 + 2 * b : 5 + 2 * b], ytab[5 + 2 * b : 6 + 2 * b])
        for h in range(6):
            four = ztab[4 * h : 4 * h + 4]
            groups.append(jnp.concatenate([four, four], axis=0) * wave)
    groups += [ztab[8 * g : 8 * g + 8] for g in range(3)]
    return groups + [first_rows(jnp.concatenate([ytab[4:8], ytab[0:4]], axis=0))]


def store_wide(xturns, ytab, e_ref, at):
    groups = wide_rows(table(xturns, "x"), ytab)
    for n in range(0, 16, 2):
        two = jnp.concatenate(groups[n : n + 2], axis=0)
        high = two.astype(bf16)
        e_ref[8 * n : 8 * n + 16, at] = high
        e_ref[128 + 8 * n : 128 + 8 * n + 16, at] = (two - high.astype(f32)).astype(bf16)


def wide_code(lane):
    group, low = lane >> 3, lane & 7
    p = jnp.where(group < 12, 4 * (group >> 2), 4 * (group - 12)) + (low & 3) + 1
    p = jnp.where(group < 15, p, 0)
    a = jnp.where(group < 12, 1 + ((group >> 1) & 1), 0)
    a = jnp.where((group == 15) & (low < 4), 1 + (low >> 1), a)
    return p, a, lane < 125


def wide_masks(lane):
    group, low = lane >> 3, lane & 7
    m_x = jnp.where(group < 15, 4, 0)
    m_a = jnp.where(group < 12, 8, jnp.where((group == 15) & (low < 4), 1, 0))
    s_x = jnp.where((low & 4) != 0, 1.0, -1.0)
    s_a = jnp.where(jnp.where(group < 12, group & 1, low & 1) != 0, 1.0, -1.0)
    return m_x, m_a, s_x, s_a


def tall_code(group, sub):
    mixed, plain = group < 12, group < 15
    r = jnp.where(mixed, 2 * (group % 6) + (sub & 1) + 1, 4 * (group - 12) + 2 * (sub >> 2) + (sub & 1) + 1)
    r = jnp.where(plain, r, 0)
    b = jnp.where(mixed, 1 + group // 6, jnp.where(plain, 0, jnp.where(sub < 4, 1 + (sub >> 1), 0)))
    return b, r, plain | (sub < 5)


def tall_masks(group, sub):
    mixed, plain = group < 12, group < 15
    m_b = jnp.where(mixed, 4, jnp.where(plain, 0, jnp.where(sub < 4, 1, 0)))
    m_z = jnp.where(plain, 2 + 0 * sub, 0)
    s_b = jnp.where(jnp.where(mixed, sub & 4, sub & 1) != 0, 1.0, -1.0)
    s_z = jnp.where((sub & 2) != 0, 1.0, -1.0)
    return m_b, m_z, s_b, s_z


def valid_row(count_ref, atoms):
    slot = lax.broadcasted_iota(jnp.int32, (1, atoms), 1)
    return (slot < count_ref[0]).astype(f32)


def prep_kernel(count_ref, pos_hbm, feat_hbm, pay_ref, pos_ref, feat_ref, sems):
    copies = [
        pltpu.make_async_copy(feat_hbm, feat_ref, sems.at[0]),
        pltpu.make_async_copy(pos_hbm, pos_ref, sems.at[1]),
    ]
    for copy in copies:
        copy.start()
    for copy in copies:
        copy.wait()
    atoms = pos_ref.shape[1]
    masked = feat_ref[...].astype(f32) * valid_row(count_ref, atoms)
    level = jnp.floor(masked * (feature_steps / feature_top) + 0.5).astype(jnp.int32)
    below = jnp.concatenate([level[2:], level[:2]], axis=0)
    words = (level << 16) | (below & 0xFFFF)
    x, y, z = (
        jnp.clip(jnp.floor(pos_ref[i : i + 1, :] * (2.0**bits / box_length) + 0.5).astype(jnp.int32), 0, 2**bits - 1)
        for i, bits in enumerate((21, 21, 22))
    )
    place = jnp.concatenate([(x << 11) | (y >> 10), ((y & 1023) << 22) | z], axis=0)
    for g in range(pay_ref.shape[0]):
        pay_ref[g] = jnp.concatenate([words[4 * g : 4 * g + 2], place], axis=0)


def unpack_turns(in_ref, turns_ref):
    first, second = in_ref[:, 2, :], in_ref[:, 3, :]
    turns_ref[0] = lax.shift_right_logical(first, 11).astype(f32) * 2.0**-21
    turns_ref[1] = (((first & 2047) << 10) | lax.shift_right_logical(second, 22)).astype(f32) * 2.0**-21
    turns_ref[2] = (second & (2**22 - 1)).astype(f32) * 2.0**-22


def faces_kernel(count_ref, core_ref, pos_ref, feat_ref, idx_ref, after_ref, flip_ref, step_ref):
    del after_ref
    atoms = pos_ref.shape[1]
    ghost = idx_ref.shape[1] // 2
    masked = feat_ref[...].astype(f32) * valid_row(count_ref, atoms)
    tail = jnp.concatenate([pos_ref[...], jnp.zeros((1, atoms), f32)], axis=0)
    hi = tail.astype(bf16).astype(f32)
    mid = (tail - hi).astype(bf16).astype(f32)
    lo = (tail - hi) - mid
    parts = jnp.concatenate([masked, hi, mid, lo, jnp.zeros((4, atoms), f32)], axis=0).astype(bf16)
    half = 2 * ghost
    row = lax.broadcasted_iota(jnp.int32, (half, ghost), 0)
    faces = []
    for n in range(2):
        want = idx_ref[0:1, n * ghost : (n + 1) * ghost] - n * half
        pick = (row == want).astype(f32).astype(bf16)
        got = jnp.dot(parts[:, n * half : (n + 1) * half], pick, preferred_element_type=f32)
        place = (got[32:36] + got[36:40]) + got[40:44]
        faces.append(jnp.concatenate([got[0:32], place, jnp.zeros((4, ghost), f32)], axis=0))
    first = core_ref[0] == 0
    flip_ref[...] = jnp.where(first, faces[1], faces[0])
    step_ref[...] = jnp.where(first, faces[0], faces[1])


def factor_kernel(in_ref, out_ref, e_ref, m_ref, turns_ref, line_ref):
    blocks, _, atoms = in_ref.shape
    unpack_turns(in_ref, turns_ref)
    for i in range(2):
        word = in_ref[:, i, :]
        line_ref[i] = (word >> 16).astype(f32) * (feature_top / feature_steps)
        line_ref[2 + i] = ((word << 16) >> 16).astype(f32) * (feature_top / feature_steps)
    total = None
    for k in range(blocks):
        cols = slice(k * atoms, (k + 1) * atoms)
        ytab = table(turns_ref[1, k : k + 1, :], "y")
        store_wide(turns_ref[0, k : k + 1, :], ytab, e_ref, cols)
        groups = tall_rows(table(turns_ref[2, k : k + 1, :], "z"), ytab)
        for c in range(4):
            line = line_ref[c, k : k + 1, :]
            for n in range(0, 16, 2):
                at = 128 * c + 8 * n
                m_ref[at : at + 16, cols] = jnp.concatenate([line * groups[n], line * groups[n + 1]], axis=0).astype(bf16)
        if k % 2:
            cols = slice((k - 1) * atoms, (k + 1) * atoms)
            dims = (((1,), (1,)), ((), ()))
            term = lax.dot_general(m_ref[:, cols], e_ref[:, cols], dims, preferred_element_type=f32)
            total = term if total is None else total + term
    out_ref[...] = (total[:, 0:128] + total[:, 128:256]).astype(bf16)


def coef_kernel(where_ref, kvec_ref, screen_ref, after_ref, out_ref):
    del after_ref
    owner = where_ref[0]
    group = owner % 16
    chan = 4 * where_ref[1] + owner // 16

    p_c, a_c, used_c = wide_code(lax.broadcasted_iota(jnp.int32, (128, 1), 0))
    code_c = jnp.where(used_c, 4 * p_c + a_c, -1)
    b_r, r_r, used_r = tall_code(group, lax.broadcasted_iota(jnp.int32, (8, 1), 0))
    code_r = jnp.where(used_r, 4 * r_r + b_r, -1)
    width = 1024
    counts = jnp.zeros((64, 128), f32)
    for n in range(kvec_ref.shape[1] // width):
        at = slice(n * width, (n + 1) * width)
        kx, ky, kz = kvec_ref[0:1, at], kvec_ref[1:2, at], kvec_ref[2:3, at]
        size = jnp.abs(ky)
        turn = jnp.where(ky < 0, -1, 1)
        ka = jnp.where(size >= 8, 2, jnp.where(size >= 3, 1, 0))
        kb = turn * (size - 5 * ka)
        wide = jnp.where(code_c == 4 * jnp.abs(kx) + ka, 1.0, 0.0).astype(bf16)
        hit = jnp.where(code_r == 4 * jnp.abs(kz) + jnp.abs(kb), 1.0, 0.0)
        sx, sa, sb, sz = (jnp.clip(k, -1, 1).astype(f32) for k in (kx, turn * ka, kb, kz))
        signs = [sx * sa, sx * sb, sx * sz, sa * sb, sa * sz, sb * sz, (sx * sa) * (sb * sz)]
        lines = jnp.concatenate([hit] + [hit * sign for sign in signs], axis=0).astype(bf16)
        counts = counts + lax.dot_general(lines, wide, (((1,), (1,)), ((), ())), preferred_element_type=f32)
    n_0, n_xa, n_xb, n_xz, n_ab, n_az, n_bz, n_all = (counts[8 * v : 8 * v + 8] for v in range(8))

    lane = lax.broadcasted_iota(jnp.int32, (8, 128), 1)
    sub = lax.broadcasted_iota(jnp.int32, (8, 128), 0)
    p, a, used_l = wide_code(lane)
    b, r, used_s = tall_code(group, sub)
    _, _, s_x, s_a = wide_masks(lane)
    _, _, s_b, s_z = tall_masks(group, sub)
    unit = 2.0 * math.pi / box_length
    screen = unit * screen_ref[pl.ds(chan, 1), :]
    screen = screen * screen

    def filt(q):
        return 1.0 / (1.0 + (p * p + q * q + r * r).astype(f32) * screen)

    like, unlike = filt(5 * a + b), filt(5 * a - b)
    used = used_l & used_s
    mean = jnp.where(used, 0.5 * (like + unlike), 0.0)
    half = jnp.where(used, 0.5 * (like - unlike), 0.0)
    out_ref[0] = mean * n_0 + half * n_ab
    out_ref[1] = -(s_x * s_a) * (mean * n_xa + half * n_xb)
    out_ref[2] = -(s_x * s_b) * (mean * n_xb + half * n_xa)
    out_ref[3] = -(s_x * s_z) * (mean * n_xz + half * n_all)
    out_ref[4] = -(s_a * s_b) * (mean * n_ab + half * n_0)
    out_ref[5] = -(s_a * s_z) * (mean * n_az + half * n_bz)
    out_ref[6] = -(s_b * s_z) * (mean * n_bz + half * n_az)
    out_ref[7] = (s_x * s_a) * (s_b * s_z) * (mean * n_all + half * n_xz)


def owner_kernel(where_ref, part_ref, coef_ref, step_ref, g1_ref, out_ref, step_out):
    del g1_ref
    step_out[...] = step_ref[...]
    group = where_ref[0] % 16
    totals = [part_ref[16 * n : 16 * n + 16, :].astype(f32) for n in range(4)]
    for n in range(4, part_ref.shape[0] // 16):
        totals[n % 4] = totals[n % 4] + part_ref[16 * n : 16 * n + 16, :].astype(f32)
    total = (totals[0] + totals[1]) + (totals[2] + totals[3])
    total = total[0:8] + total[8:16]
    lane = lax.broadcasted_iota(jnp.int32, (8, 128), 1)
    sub = lax.broadcasted_iota(jnp.int32, (8, 128), 0)
    m_x, m_a, _, _ = wide_masks(lane)
    m_b, m_z, _, _ = tall_masks(group, sub)

    def lanes(value, mask):
        return jnp.take_along_axis(value, lane ^ mask, axis=1)

    def rows(value, mask):
        return jnp.take_along_axis(value, sub ^ mask, axis=0)

    t_x, t_a, t_xa = lanes(total, m_x), lanes(total, m_a), lanes(total, m_x ^ m_a)
    terms = [
        total,
        t_xa,
        rows(t_x, m_b),
        rows(t_x, m_z),
        rows(t_a, m_b),
        rows(t_a, m_z),
        rows(total, m_b ^ m_z),
        rows(t_xa, m_b ^ m_z),
    ]
    done = coef_ref[0] * terms[0]
    for n in range(1, 8):
        done = done + coef_ref[n] * terms[n]
    twice = jnp.concatenate([done, done], axis=0).astype(bf16)
    for n in range(out_ref.shape[0] // 16):
        out_ref[16 * n : 16 * n + 16, :] = twice


def field_blocks(first, filt_ref, in_ref, out_ref, e_ref, g_ref, turns_ref):
    unpack_turns(in_ref, turns_ref)
    rows = filt_ref.shape[0]
    late = 8 * (first_out - first_in) % rows
    for at in (0, 128):
        g_ref[late:rows, at : at + 128] = filt_ref[0 : rows - late, :]
        if late:
            g_ref[0:late, at : at + 128] = filt_ref[rows - late : rows, :]
    atoms = out_ref.shape[2]
    for k in range(first, out_ref.shape[0]):
        cols = slice((k - first) * atoms, (k - first + 1) * atoms)
        ytab = table(turns_ref[1, k : k + 1, :], "y")
        store_wide(turns_ref[0, k : k + 1, :], ytab, e_ref, cols)
        groups = tall_rows(table(turns_ref[2, k : k + 1, :], "z"), ytab)
        term = jnp.dot(g_ref[...], e_ref[:, cols], preferred_element_type=f32)
        lines = []
        for c in range(4):
            acc = term[128 * c : 128 * c + 8] * groups[0]
            for n in range(1, 16):
                acc = acc + term[128 * c + 8 * n : 128 * c + 8 * n + 8] * groups[n]
            lines.append(jnp.sum(acc, axis=0, keepdims=True))
        out_ref[k] = jnp.concatenate(lines, axis=0)


def field_kernel(filt_ref, in_ref, out_ref, e_ref, g_ref, turns_ref):
    field_blocks(0, filt_ref, in_ref, out_ref, e_ref, g_ref, turns_ref)


def rest_kernel(filt_ref, in_ref, part_ref, g2_ref, out_ref, e_ref, g_ref, turns_ref):
    del g2_ref
    done = part_ref.shape[0]
    out_ref[0:done] = part_ref[...]
    field_blocks(done, filt_ref, in_ref, out_ref, e_ref, g_ref, turns_ref)


shrink = math.sqrt(math.log2(math.e) / pair_scale)


def pairs(cols, rows, wrap):
    box = box_length * shrink
    dx = cols[:, 0:1] - rows[0:1]
    if wrap:
        dx = jnp.abs(dx)
        dx = jnp.minimum(dx, box - dx)
    dy = cols[:, 1:2] - rows[1:2]
    dz = jnp.abs(cols[:, 2:3] - rows[2:3])
    dz = jnp.minimum(dz, box - dz)
    return jnp.exp2(-(dx * dx + dy * dy + dz * dz)).astype(bf16)


def short_kernel(
    count_ref, pos_ref, feat_ref, g1_ref, g2_ref, lw_ref, sw_ref, after_ref, base_ref, twice_ref
):
    del after_ref
    atoms = pos_ref.shape[1]
    feat = feat_ref[...].astype(f32)
    masked = (feat * valid_row(count_ref, atoms)).astype(bf16)
    rows = pos_ref[...] * shrink
    rows8 = jnp.concatenate([rows, jnp.zeros((5, atoms), f32)], axis=0)
    ghost = jnp.concatenate([g1_ref[...], g2_ref[...]], axis=1)
    near_by = pairs(jnp.transpose(ghost[32:40] * shrink), rows, True)
    short = jnp.dot(ghost[0:32].astype(bf16), near_by, preferred_element_type=f32)
    step = 256
    for n in range(atoms // step):
        at = slice(n * step, (n + 1) * step)
        own = pairs(jnp.transpose(rows8[:, at]), rows, False)
        short = short + jnp.dot(masked[:, at], own, preferred_element_type=f32)
    mixed = jnp.dot(stacked(sw_ref[...]), split(short), preferred_element_type=f32)
    base_ref[...] = feat + short_gain * mixed
    twice_ref[...] = stacked(lw_ref[...])


def stacked(weight):
    turned = jnp.transpose(weight.astype(f32))
    return jnp.concatenate([turned, turned], axis=1).astype(bf16)


def split(value):
    high = value.astype(bf16)
    low = (value - high.astype(f32)).astype(bf16)
    return jnp.concatenate([high, low], axis=0)


def final_kernel(count_ref, base_ref, long_ref, twice_ref, out_ref, *, long_scale):
    mixed = jnp.dot(twice_ref[...], split(long_ref[...]), preferred_element_type=f32)
    total = base_ref[...] + long_scale * mixed
    out_ref[...] = (total * valid_row(count_ref, total.shape[1])).astype(bf16)


def swap_parts(parts, axis, first):
    count = parts.shape[0]
    order = [[(n + first) % count for n in range(count)]]
    return lax.all_to_all(parts, axis, 0, 0, axis_index_groups=order, tiled=True)


def whole(memory=pltpu.VMEM):
    return pl.BlockSpec(memory_space=memory)


def local(positions, features, counts, ghost_index, kvec, screen_len, long_weight, short_weight):
    chans, atoms = features.shape
    total_vec = kvec.shape[1]
    ghost = ghost_index.shape[1] // 2
    near = lax.axis_size(NEAR)
    far = lax.axis_size(FAR)
    params = pltpu.CompilerParams(vmem_limit_bytes=vmem_limit)

    payload = pl.pallas_call(
        prep_kernel,
        name="prep",
        out_shape=jax.ShapeDtypeStruct((near, 4, atoms), jnp.int32),
        in_specs=[whole(pltpu.SMEM), whole(pl.ANY), whole(pl.ANY)],
        out_specs=whole(),
        scratch_shapes=[
            pltpu.VMEM(positions.shape, f32),
            pltpu.VMEM(features.shape, bf16),
            pltpu.SemaphoreType.DMA((2,)),
        ],
    )(counts, positions, features)
    gathered = swap_parts(payload, NEAR, first_near)

    rows = jax.ShapeDtypeStruct((8 * far, 128), bf16)

    def exchange(value, first):
        parts = value.reshape(far, 8, 128)
        return swap_parts(parts, FAR, first).reshape(8 * far, 128)

    partial = pl.pallas_call(
        factor_kernel,
        name="factor",
        out_shape=rows,
        in_specs=[whole()],
        out_specs=whole(),
        scratch_shapes=[
            pltpu.VMEM((256, near * atoms), bf16),
            pltpu.VMEM((512, near * atoms), bf16),
            pltpu.VMEM((3, near, atoms), f32),
            pltpu.VMEM((4, near, atoms), f32),
        ],
        compiler_params=params,
    )(gathered)
    spread = exchange(partial, first_in)

    owner = (lax.axis_index(FAR) + far - first_in) % far
    share = (lax.axis_index(NEAR) + near - first_near) % near
    place = jnp.stack([owner, share]).astype(jnp.int32)
    screens = jnp.broadcast_to(screen_len[:, None], (chans, 128))
    coef = pl.pallas_call(
        coef_kernel,
        name="coef",
        out_shape=jax.ShapeDtypeStruct((8, 8, 128), f32),
        in_specs=[whole(pltpu.SMEM), whole(), whole(), whole(pl.ANY)],
        out_specs=whole(),
        compiler_params=params,
        cost_estimate=pl.CostEstimate(flops=2 * 64 * 256 * total_vec, bytes_accessed=8 * total_vec, transcendentals=0),
    )(place, kvec, screens, partial)
    core = lax.axis_index("core").reshape(1).astype(jnp.int32)
    face = jax.ShapeDtypeStruct((chans + 8, ghost), f32)
    flip_face, step_face = pl.pallas_call(
        faces_kernel,
        name="faces",
        out_shape=[face, face],
        in_specs=[whole(pltpu.SMEM), whole(pltpu.SMEM), whole(), whole(), whole(), whole(pl.ANY)],
        out_specs=[whole(), whole()],
        compiler_params=params,
    )(counts, core, positions, features, ghost_index, partial)
    n_dom = lax.axis_size(DOM)
    flip = [(d, d ^ 1) for d in range(n_dom)]
    step = [(d, (d + 1) % n_dom if d % 2 else (d - 1) % n_dom) for d in range(n_dom)]
    ghosts_1 = lax.ppermute(flip_face, DOM, flip)
    filtered, step_face = pl.pallas_call(
        owner_kernel,
        name="owner",
        out_shape=[rows, face],
        in_specs=[whole(pltpu.SMEM)] + [whole()] * 3 + [whole(pl.ANY)],
        out_specs=[whole()] * 2,
        compiler_params=params,
    )(place, spread, coef, step_face, ghosts_1)
    everywhere = exchange(filtered, first_out)
    ghosts_2 = lax.ppermute(step_face, DOM, step)
    early = near * 3 // 4
    field_scratch = [
        pltpu.VMEM((256, max(early, near - early) * atoms), bf16),
        pltpu.VMEM((512, 256), bf16),
        pltpu.VMEM((3, near, atoms), f32),
    ]
    field = pl.pallas_call(
        field_kernel,
        name="field",
        out_shape=jax.ShapeDtypeStruct((early, 4, atoms), f32),
        in_specs=[whole()] * 2,
        out_specs=whole(),
        scratch_shapes=field_scratch,
        compiler_params=params,
    )(everywhere, gathered)
    field = pl.pallas_call(
        rest_kernel,
        name="rest",
        out_shape=jax.ShapeDtypeStruct((near, 4, atoms), f32),
        in_specs=[whole()] * 3 + [whole(pl.ANY)],
        out_specs=whole(),
        scratch_shapes=field_scratch,
        compiler_params=params,
    )(everywhere, gathered, field, ghosts_2)
    base, twice = pl.pallas_call(
        short_kernel,
        name="short",
        out_shape=[jax.ShapeDtypeStruct((chans, atoms), f32), jax.ShapeDtypeStruct((chans, 2 * chans), bf16)],
        in_specs=[whole(pltpu.SMEM)] + [whole()] * 6 + [whole(pl.ANY)],
        out_specs=[whole()] * 2,
        compiler_params=params,
        cost_estimate=pl.CostEstimate(flops=2 * 256 * 1280 * atoms, bytes_accessed=10 * 32 * atoms, transcendentals=1280 * atoms),
    )(counts, positions, features, ghosts_1, ghosts_2, long_weight, short_weight, field)
    longmsg = swap_parts(field, NEAR, first_near).reshape(chans, atoms)
    all_atoms = atoms * lax.axis_size(ALL)
    long_scale = long_gain / math.sqrt(total_vec * all_atoms)
    return pl.pallas_call(
        lambda *refs: final_kernel(*refs, long_scale=long_scale),
        name="final",
        out_shape=jax.ShapeDtypeStruct((chans, atoms), bf16),
        in_specs=[whole(pltpu.SMEM)] + [whole()] * 3,
        out_specs=whole(),
        compiler_params=params,
    )(counts, base, longmsg, twice)


def solution(mesh):
    fine = Mesh(mesh.devices.reshape(4, 2, 2, 8, 4), ALL)
    return jax.shard_map(
        local,
        mesh=fine,
        in_specs=(P(None, ALL), P(None, ALL), P(ALL), P(ALL, None), P(), P(), P(), P()),
        out_specs=P(None, ALL),
        check_vma=False,
    )
```

```python
import math

import jax
import jax.numpy as jnp
import numpy as np
from jax import lax
from jax.experimental import pallas as pl
from jax.experimental.pallas import tpu as pltpu
from jax.sharding import Mesh, PartitionSpec as P

box_length = 216.0
pair_scale = 12.5
short_gain = 0.5
long_gain = 16.0
feature_top = 6.0
feature_steps = 32767.0
first_in = 59
first_out = 59
first_near = 4
vmem_limit = 48 * 1024 * 1024

ALL = ("x", "zh", "core", "y", "zl")
DOM = ("x", "zh", "core")
NEAR = ("x", "core")
FAR = ("zh", "y", "zl")

f32 = jnp.float32
bf16 = jnp.bfloat16


def fit_cos(degree):
    nodes = np.cos(np.pi * (np.arange(64) + 0.5) / 64)
    w = 0.125 * (nodes + 1.0)
    cheb = np.polynomial.chebyshev.Chebyshev.fit(w, np.cos(2 * np.pi * np.sqrt(w)), degree, domain=[0.0, 0.25])
    return [float(c) for c in cheb.convert(kind=np.polynomial.Polynomial).coef]


COS_POLY = fit_cos(6)


def turn_cos(v):
    r = v - jnp.floor(v + 0.5)
    w = r * r
    acc = w * COS_POLY[-1] + COS_POLY[-2]
    for c in COS_POLY[-3::-1]:
        acc = acc * w + c
    return acc


def table(turns, kind):
    row = lax.broadcasted_iota(jnp.int32, (8 if kind == "y" else 24, 1), 0)
    if kind == "x":
        freq = 4 * (row >> 3) + (row & 3) + 1
        sine = (row & 4) != 0
    elif kind == "z":
        freq = 2 * (row >> 2) + (row & 1) + 1
        sine = (row & 2) != 0
    else:
        freq = jnp.where(row < 2, 5, jnp.where(row < 4, 10, jnp.where(row < 6, 1, 2)))
        sine = (row & 1) != 0
    return turn_cos(freq.astype(f32) * turns - jnp.where(sine, 0.25, 0.0))


def first_rows(rows):
    sub = lax.broadcasted_iota(jnp.int32, rows.shape, 0)
    return jnp.where(sub < 4, rows, jnp.where(sub == 4, 1.0, 0.0))


def wide_rows(xtab, ytab):
    groups = []
    for g in range(3):
        groups += [xtab[8 * g : 8 * g + 8] * ytab[f : f + 1] for f in range(4)]
    groups += [xtab[8 * g : 8 * g + 8] for g in range(3)]
    return groups + [first_rows(ytab)]


def tall_rows(ztab, ytab):
    sub = lax.broadcasted_iota(jnp.int32, ytab.shape, 0)
    groups = []
    for b in range(2):
        wave = jnp.where(sub < 4, ytab[4 + 2 * b : 5 + 2 * b], ytab[5 + 2 * b : 6 + 2 * b])
        for h in range(6):
            four = ztab[4 * h : 4 * h + 4]
            groups.append(jnp.concatenate([four, four], axis=0) * wave)
    groups += [ztab[8 * g : 8 * g + 8] for g in range(3)]
    return groups + [first_rows(jnp.concatenate([ytab[4:8], ytab[0:4]], axis=0))]


def store_wide(xturns, ytab, e_ref, at):
    groups = wide_rows(table(xturns, "x"), ytab)
    for n in range(0, 16, 2):
        two = jnp.concatenate(groups[n : n + 2], axis=0)
        high = two.astype(bf16)
        e_ref[8 * n : 8 * n + 16, at] = high
        e_ref[128 + 8 * n : 128 + 8 * n + 16, at] = (two - high.astype(f32)).astype(bf16)


def wide_code(lane):
    group, low = lane >> 3, lane & 7
    p = jnp.where(group < 12, 4 * (group >> 2), 4 * (group - 12)) + (low & 3) + 1
    p = jnp.where(group < 15, p, 0)
    a = jnp.where(group < 12, 1 + ((group >> 1) & 1), 0)
    a = jnp.where((group == 15) & (low < 4), 1 + (low >> 1), a)
    return p, a, lane < 125


def wide_masks(lane):
    group, low = lane >> 3, lane & 7
    m_x = jnp.where(group < 15, 4, 0)
    m_a = jnp.where(group < 12, 8, jnp.where((group == 15) & (low < 4), 1, 0))
    s_x = jnp.where((low & 4) != 0, 1.0, -1.0)
    s_a = jnp.where(jnp.where(group < 12, group & 1, low & 1) != 0, 1.0, -1.0)
    return m_x, m_a, s_x, s_a


def tall_code(group, sub):
    mixed, plain = group < 12, group < 15
    r = jnp.where(mixed, 2 * (group % 6) + (sub & 1) + 1, 4 * (group - 12) + 2 * (sub >> 2) + (sub & 1) + 1)
    r = jnp.where(plain, r, 0)
    b = jnp.where(mixed, 1 + group // 6, jnp.where(plain, 0, jnp.where(sub < 4, 1 + (sub >> 1), 0)))
    return b, r, plain | (sub < 5)


def tall_masks(group, sub):
    mixed, plain = group < 12, group < 15
    m_b = jnp.where(mixed, 4, jnp.where(plain, 0, jnp.where(sub < 4, 1, 0)))
    m_z = jnp.where(plain, 2 + 0 * sub, 0)
    s_b = jnp.where(jnp.where(mixed, sub & 4, sub & 1) != 0, 1.0, -1.0)
    s_z = jnp.where((sub & 2) != 0, 1.0, -1.0)
    return m_b, m_z, s_b, s_z


def valid_row(count_ref, atoms):
    slot = lax.broadcasted_iota(jnp.int32, (1, atoms), 1)
    return (slot < count_ref[0]).astype(f32)


def prep_kernel(count_ref, pos_hbm, feat_hbm, pay_ref, pos_ref, feat_ref, sems):
    copies = [
        pltpu.make_async_copy(feat_hbm, feat_ref, sems.at[0]),
        pltpu.make_async_copy(pos_hbm, pos_ref, sems.at[1]),
    ]
    for copy in copies:
        copy.start()
    for copy in copies:
        copy.wait()
    atoms = pos_ref.shape[1]
    masked = feat_ref[...].astype(f32) * valid_row(count_ref, atoms)
    level = jnp.floor(masked * (feature_steps / feature_top) + 0.5).astype(jnp.int32)
    below = jnp.concatenate([level[2:], level[:2]], axis=0)
    words = (level << 16) | (below & 0xFFFF)
    x, y, z = (
        jnp.clip(jnp.floor(pos_ref[i : i + 1, :] * (2.0**bits / box_length) + 0.5).astype(jnp.int32), 0, 2**bits - 1)
        for i, bits in enumerate((21, 21, 22))
    )
    place = jnp.concatenate([(x << 11) | (y >> 10), ((y & 1023) << 22) | z], axis=0)
    for g in range(pay_ref.shape[0]):
        pay_ref[g] = jnp.concatenate([words[4 * g : 4 * g + 2], place], axis=0)


def unpack_turns(in_ref, turns_ref):
    first, second = in_ref[:, 2, :], in_ref[:, 3, :]
    turns_ref[0] = lax.shift_right_logical(first, 11).astype(f32) * 2.0**-21
    turns_ref[1] = (((first & 2047) << 10) | lax.shift_right_logical(second, 22)).astype(f32) * 2.0**-21
    turns_ref[2] = (second & (2**22 - 1)).astype(f32) * 2.0**-22


def faces_kernel(count_ref, core_ref, pos_ref, feat_ref, idx_ref, after_ref, flip_ref, step_ref):
    del after_ref
    atoms = pos_ref.shape[1]
    ghost = idx_ref.shape[1] // 2
    masked = feat_ref[...].astype(f32) * valid_row(count_ref, atoms)
    tail = jnp.concatenate([pos_ref[...], jnp.zeros((1, atoms), f32)], axis=0)
    hi = tail.astype(bf16).astype(f32)
    mid = (tail - hi).astype(bf16).astype(f32)
    lo = (tail - hi) - mid
    parts = jnp.concatenate([masked, hi, mid, lo, jnp.zeros((4, atoms), f32)], axis=0).astype(bf16)
    half = 2 * ghost
    row = lax.broadcasted_iota(jnp.int32, (half, ghost), 0)
    faces = []
    for n in range(2):
        want = idx_ref[0:1, n * ghost : (n + 1) * ghost] - n * half
        pick = (row == want).astype(f32).astype(bf16)
        got = jnp.dot(parts[:, n * half : (n + 1) * half], pick, preferred_element_type=f32)
        place = (got[32:36] + got[36:40]) + got[40:44]
        faces.append(jnp.concatenate([got[0:32], place, jnp.zeros((4, ghost), f32)], axis=0))
    first = core_ref[0] == 0
    flip_ref[...] = jnp.where(first, faces[1], faces[0])
    step_ref[...] = jnp.where(first, faces[0], faces[1])


def factor_kernel(in_ref, out_ref, e_ref, m_ref, turns_ref, line_ref):
    blocks, _, atoms = in_ref.shape
    unpack_turns(in_ref, turns_ref)
    for i in range(2):
        word = in_ref[:, i, :]
        line_ref[i] = (word >> 16).astype(f32) * (feature_top / feature_steps)
        line_ref[2 + i] = ((word << 16) >> 16).astype(f32) * (feature_top / feature_steps)
    total = None
    for k in range(blocks):
        cols = slice(k * atoms, (k + 1) * atoms)
        ytab = table(turns_ref[1, k : k + 1, :], "y")
        store_wide(turns_ref[0, k : k + 1, :], ytab, e_ref, cols)
        groups = tall_rows(table(turns_ref[2, k : k + 1, :], "z"), ytab)
        for c in range(4):
            line = line_ref[c, k : k + 1, :]
            for n in range(0, 16, 2):
                at = 128 * c + 8 * n
                m_ref[at : at + 16, cols] = jnp.concatenate([line * groups[n], line * groups[n + 1]], axis=0).astype(bf16)
        if k % 2:
            cols = slice((k - 1) * atoms, (k + 1) * atoms)
            dims = (((1,), (1,)), ((), ()))
            term = lax.dot_general(m_ref[:, cols], e_ref[:, cols], dims, preferred_element_type=f32)
            total = term if total is None else total + term
    out_ref[...] = (total[:, 0:128] + total[:, 128:256]).astype(bf16)


def coef_kernel(where_ref, kvec_ref, screen_ref, after_ref, out_ref):
    del after_ref
    owner = where_ref[0]
    group = owner % 16
    chan = 4 * where_ref[1] + owner // 16

    p_c, a_c, used_c = wide_code(lax.broadcasted_iota(jnp.int32, (128, 1), 0))
    code_c = jnp.where(used_c, 4 * p_c + a_c, -1)
    b_r, r_r, used_r = tall_code(group, lax.broadcasted_iota(jnp.int32, (8, 1), 0))
    code_r = jnp.where(used_r, 4 * r_r + b_r, -1)
    width = 1024
    counts = jnp.zeros((64, 128), f32)
    for n in range(kvec_ref.shape[1] // width):
        at = slice(n * width, (n + 1) * width)
        kx, ky, kz = kvec_ref[0:1, at], kvec_ref[1:2, at], kvec_ref[2:3, at]
        size = jnp.abs(ky)
        turn = jnp.where(ky < 0, -1, 1)
        ka = jnp.where(size >= 8, 2, jnp.where(size >= 3, 1, 0))
        kb = turn * (size - 5 * ka)
        wide = jnp.where(code_c == 4 * jnp.abs(kx) + ka, 1.0, 0.0).astype(bf16)
        hit = jnp.where(code_r == 4 * jnp.abs(kz) + jnp.abs(kb), 1.0, 0.0)
        sx, sa, sb, sz = (jnp.clip(k, -1, 1).astype(f32) for k in (kx, turn * ka, kb, kz))
        signs = [sx * sa, sx * sb, sx * sz, sa * sb, sa * sz, sb * sz, (sx * sa) * (sb * sz)]
        lines = jnp.concatenate([hit] + [hit * sign for sign in signs], axis=0).astype(bf16)
        counts = counts + lax.dot_general(lines, wide, (((1,), (1,)), ((), ())), preferred_element_type=f32)
    n_0, n_xa, n_xb, n_xz, n_ab, n_az, n_bz, n_all = (counts[8 * v : 8 * v + 8] for v in range(8))

    lane = lax.broadcasted_iota(jnp.int32, (8, 128), 1)
    sub = lax.broadcasted_iota(jnp.int32, (8, 128), 0)
    p, a, used_l = wide_code(lane)
    b, r, used_s = tall_code(group, sub)
    _, _, s_x, s_a = wide_masks(lane)
    _, _, s_b, s_z = tall_masks(group, sub)
    unit = 2.0 * math.pi / box_length
    screen = unit * screen_ref[pl.ds(chan, 1), :]
    screen = screen * screen

    def filt(q):
        return 1.0 / (1.0 + (p * p + q * q + r * r).astype(f32) * screen)

    like, unlike = filt(5 * a + b), filt(5 * a - b)
    used = used_l & used_s
    mean = jnp.where(used, 0.5 * (like + unlike), 0.0)
    half = jnp.where(used, 0.5 * (like - unlike), 0.0)
    out_ref[0] = mean * n_0 + half * n_ab
    out_ref[1] = -(s_x * s_a) * (mean * n_xa + half * n_xb)
    out_ref[2] = -(s_x * s_b) * (mean * n_xb + half * n_xa)
    out_ref[3] = -(s_x * s_z) * (mean * n_xz + half * n_all)
    out_ref[4] = -(s_a * s_b) * (mean * n_ab + half * n_0)
    out_ref[5] = -(s_a * s_z) * (mean * n_az + half * n_bz)
    out_ref[6] = -(s_b * s_z) * (mean * n_bz + half * n_az)
    out_ref[7] = (s_x * s_a) * (s_b * s_z) * (mean * n_all + half * n_xz)


def owner_kernel(where_ref, part_ref, coef_ref, step_ref, g1_ref, out_ref, step_out):
    del g1_ref
    step_out[...] = step_ref[...]
    group = where_ref[0] % 16
    totals = [part_ref[16 * n : 16 * n + 16, :].astype(f32) for n in range(4)]
    for n in range(4, part_ref.shape[0] // 16):
        totals[n % 4] = totals[n % 4] + part_ref[16 * n : 16 * n + 16, :].astype(f32)
    total = (totals[0] + totals[1]) + (totals[2] + totals[3])
    total = total[0:8] + total[8:16]
    lane = lax.broadcasted_iota(jnp.int32, (8, 128), 1)
    sub = lax.broadcasted_iota(jnp.int32, (8, 128), 0)
    m_x, m_a, _, _ = wide_masks(lane)
    m_b, m_z, _, _ = tall_masks(group, sub)

    def lanes(value, mask):
        return jnp.take_along_axis(value, lane ^ mask, axis=1)

    def rows(value, mask):
        return jnp.take_along_axis(value, sub ^ mask, axis=0)

    t_x, t_a, t_xa = lanes(total, m_x), lanes(total, m_a), lanes(total, m_x ^ m_a)
    terms = [
        total,
        t_xa,
        rows(t_x, m_b),
        rows(t_x, m_z),
        rows(t_a, m_b),
        rows(t_a, m_z),
        rows(total, m_b ^ m_z),
        rows(t_xa, m_b ^ m_z),
    ]
    done = coef_ref[0] * terms[0]
    for n in range(1, 8):
        done = done + coef_ref[n] * terms[n]
    twice = jnp.concatenate([done, done], axis=0).astype(bf16)
    for n in range(out_ref.shape[0] // 16):
        out_ref[16 * n : 16 * n + 16, :] = twice


def field_blocks(first, filt_ref, in_ref, out_ref, e_ref, g_ref, turns_ref):
    unpack_turns(in_ref, turns_ref)
    rows = filt_ref.shape[0]
    late = 8 * (first_out - first_in) % rows
    for at in (0, 128):
        g_ref[late:rows, at : at + 128] = filt_ref[0 : rows - late, :]
        if late:
            g_ref[0:late, at : at + 128] = filt_ref[rows - late : rows, :]
    atoms = out_ref.shape[2]
    for k in range(first, out_ref.shape[0]):
        cols = slice((k - first) * atoms, (k - first + 1) * atoms)
        ytab = table(turns_ref[1, k : k + 1, :], "y")
        store_wide(turns_ref[0, k : k + 1, :], ytab, e_ref, cols)
        groups = tall_rows(table(turns_ref[2, k : k + 1, :], "z"), ytab)
        term = jnp.dot(g_ref[...], e_ref[:, cols], preferred_element_type=f32)
        lines = []
        for c in range(4):
            acc = term[128 * c : 128 * c + 8] * groups[0]
            for n in range(1, 16):
                acc = acc + term[128 * c + 8 * n : 128 * c + 8 * n + 8] * groups[n]
            lines.append(jnp.sum(acc, axis=0, keepdims=True))
        out_ref[k] = jnp.concatenate(lines, axis=0)


def field_kernel(filt_ref, in_ref, own_ref, out_ref, e_ref, g_ref, turns_ref):
    del own_ref
    field_blocks(0, filt_ref, in_ref, out_ref, e_ref, g_ref, turns_ref)


def rest_kernel(filt_ref, in_ref, part_ref, g2_ref, out_ref, e_ref, g_ref, turns_ref):
    del g2_ref
    done = part_ref.shape[0]
    out_ref[0:done] = part_ref[...]
    field_blocks(done, filt_ref, in_ref, out_ref, e_ref, g_ref, turns_ref)


shrink = math.sqrt(math.log2(math.e) / pair_scale)


def pairs(cols, rows, wrap):
    box = box_length * shrink
    dx = cols[:, 0:1] - rows[0:1]
    if wrap:
        dx = jnp.abs(dx)
        dx = jnp.minimum(dx, box - dx)
    dy = cols[:, 1:2] - rows[1:2]
    dz = jnp.abs(cols[:, 2:3] - rows[2:3])
    dz = jnp.minimum(dz, box - dz)
    return jnp.exp2(-(dx * dx + dy * dy + dz * dz)).astype(bf16)


def own_kernel(count_ref, pos_ref, feat_ref, after_ref, out_ref):
    del after_ref
    atoms = pos_ref.shape[1]
    masked = (feat_ref[...].astype(f32) * valid_row(count_ref, atoms)).astype(bf16)
    rows = pos_ref[...] * shrink
    rows8 = jnp.concatenate([rows, jnp.zeros((5, atoms), f32)], axis=0)
    step = 256
    total = None
    for n in range(atoms // step):
        at = slice(n * step, (n + 1) * step)
        term = jnp.dot(masked[:, at], pairs(jnp.transpose(rows8[:, at]), rows, False), preferred_element_type=f32)
        total = term if total is None else total + term
    out_ref[...] = total


def short_kernel(pos_ref, feat_ref, g1_ref, g2_ref, own_ref, lw_ref, sw_ref, after_ref, base_ref, twice_ref):
    del after_ref
    ghost = jnp.concatenate([g1_ref[...], g2_ref[...]], axis=1)
    near_by = pairs(jnp.transpose(ghost[32:40] * shrink), pos_ref[...] * shrink, True)
    short = own_ref[...] + jnp.dot(ghost[0:32].astype(bf16), near_by, preferred_element_type=f32)
    mixed = jnp.dot(stacked(sw_ref[...]), split(short), preferred_element_type=f32)
    base_ref[...] = feat_ref[...].astype(f32) + short_gain * mixed
    twice_ref[...] = stacked(lw_ref[...])


def stacked(weight):
    turned = jnp.transpose(weight.astype(f32))
    return jnp.concatenate([turned, turned], axis=1).astype(bf16)


def split(value):
    high = value.astype(bf16)
    low = (value - high.astype(f32)).astype(bf16)
    return jnp.concatenate([high, low], axis=0)


def final_kernel(count_ref, base_ref, long_ref, twice_ref, out_ref, *, long_scale):
    mixed = jnp.dot(twice_ref[...], split(long_ref[...]), preferred_element_type=f32)
    total = base_ref[...] + long_scale * mixed
    out_ref[...] = (total * valid_row(count_ref, total.shape[1])).astype(bf16)


def swap_parts(parts, axis, first):
    count = parts.shape[0]
    order = [[(n + first) % count for n in range(count)]]
    return lax.all_to_all(parts, axis, 0, 0, axis_index_groups=order, tiled=True)


def whole(memory=pltpu.VMEM):
    return pl.BlockSpec(memory_space=memory)


def local(positions, features, counts, ghost_index, kvec, screen_len, long_weight, short_weight):
    chans, atoms = features.shape
    total_vec = kvec.shape[1]
    ghost = ghost_index.shape[1] // 2
    near = lax.axis_size(NEAR)
    far = lax.axis_size(FAR)
    params = pltpu.CompilerParams(vmem_limit_bytes=vmem_limit)

    payload = pl.pallas_call(
        prep_kernel,
        name="prep",
        out_shape=jax.ShapeDtypeStruct((near, 4, atoms), jnp.int32),
        in_specs=[whole(pltpu.SMEM), whole(pl.ANY), whole(pl.ANY)],
        out_specs=whole(),
        scratch_shapes=[
            pltpu.VMEM(positions.shape, f32),
            pltpu.VMEM(features.shape, bf16),
            pltpu.SemaphoreType.DMA((2,)),
        ],
    )(counts, positions, features)
    gathered = swap_parts(payload, NEAR, first_near)

    rows = jax.ShapeDtypeStruct((8 * far, 128), bf16)

    def exchange(value, first):
        parts = value.reshape(far, 8, 128)
        return swap_parts(parts, FAR, first).reshape(8 * far, 128)

    partial = pl.pallas_call(
        factor_kernel,
        name="factor",
        out_shape=rows,
        in_specs=[whole()],
        out_specs=whole(),
        scratch_shapes=[
            pltpu.VMEM((256, near * atoms), bf16),
            pltpu.VMEM((512, near * atoms), bf16),
            pltpu.VMEM((3, near, atoms), f32),
            pltpu.VMEM((4, near, atoms), f32),
        ],
        compiler_params=params,
    )(gathered)
    spread = exchange(partial, first_in)

    owner = (lax.axis_index(FAR) + far - first_in) % far
    share = (lax.axis_index(NEAR) + near - first_near) % near
    place = jnp.stack([owner, share]).astype(jnp.int32)
    screens = jnp.broadcast_to(screen_len[:, None], (chans, 128))
    coef = pl.pallas_call(
        coef_kernel,
        name="coef",
        out_shape=jax.ShapeDtypeStruct((8, 8, 128), f32),
        in_specs=[whole(pltpu.SMEM), whole(), whole(), whole(pl.ANY)],
        out_specs=whole(),
        compiler_params=params,
        cost_estimate=pl.CostEstimate(flops=2 * 64 * 256 * total_vec, bytes_accessed=8 * total_vec, transcendentals=0),
    )(place, kvec, screens, partial)
    core = lax.axis_index("core").reshape(1).astype(jnp.int32)
    face = jax.ShapeDtypeStruct((chans + 8, ghost), f32)
    flip_face, step_face = pl.pallas_call(
        faces_kernel,
        name="faces",
        out_shape=[face, face],
        in_specs=[whole(pltpu.SMEM), whole(pltpu.SMEM), whole(), whole(), whole(), whole(pl.ANY)],
        out_specs=[whole(), whole()],
        compiler_params=params,
    )(counts, core, positions, features, ghost_index, partial)
    n_dom = lax.axis_size(DOM)
    flip = [(d, d ^ 1) for d in range(n_dom)]
    step = [(d, (d + 1) % n_dom if d % 2 else (d - 1) % n_dom) for d in range(n_dom)]
    ghosts_1 = lax.ppermute(flip_face, DOM, flip)
    filtered, step_face = pl.pallas_call(
        owner_kernel,
        name="owner",
        out_shape=[rows, face],
        in_specs=[whole(pltpu.SMEM)] + [whole()] * 3 + [whole(pl.ANY)],
        out_specs=[whole()] * 2,
        compiler_params=params,
    )(place, spread, coef, step_face, ghosts_1)
    everywhere = exchange(filtered, first_out)
    ghosts_2 = lax.ppermute(step_face, DOM, step)
    own = pl.pallas_call(
        own_kernel,
        name="own",
        out_shape=jax.ShapeDtypeStruct((chans, atoms), f32),
        in_specs=[whole(pltpu.SMEM), whole(), whole(), whole(pl.ANY)],
        out_specs=whole(),
        compiler_params=params,
    )(counts, positions, features, filtered)
    early = near * 7 // 8
    field_scratch = [
        pltpu.VMEM((256, max(early, near - early) * atoms), bf16),
        pltpu.VMEM((512, 256), bf16),
        pltpu.VMEM((3, near, atoms), f32),
    ]
    field = pl.pallas_call(
        field_kernel,
        name="field",
        out_shape=jax.ShapeDtypeStruct((early, 4, atoms), f32),
        in_specs=[whole()] * 2 + [whole(pl.ANY)],
        out_specs=whole(),
        scratch_shapes=field_scratch,
        compiler_params=params,
    )(everywhere, gathered, own)
    field = pl.pallas_call(
        rest_kernel,
        name="rest",
        out_shape=jax.ShapeDtypeStruct((near, 4, atoms), f32),
        in_specs=[whole()] * 3 + [whole(pl.ANY)],
        out_specs=whole(),
        scratch_shapes=field_scratch,
        compiler_params=params,
    )(everywhere, gathered, field, ghosts_2)
    base, twice = pl.pallas_call(
        short_kernel,
        name="short",
        out_shape=[jax.ShapeDtypeStruct((chans, atoms), f32), jax.ShapeDtypeStruct((chans, 2 * chans), bf16)],
        in_specs=[whole()] * 7 + [whole(pl.ANY)],
        out_specs=[whole()] * 2,
        compiler_params=params,
        cost_estimate=pl.CostEstimate(flops=2 * 256 * 256 * atoms, bytes_accessed=10 * 32 * atoms, transcendentals=256 * atoms),
    )(positions, features, ghosts_1, ghosts_2, own, long_weight, short_weight, field)
    longmsg = swap_parts(field, NEAR, first_near).reshape(chans, atoms)
    all_atoms = atoms * lax.axis_size(ALL)
    long_scale = long_gain / math.sqrt(total_vec * all_atoms)
    return pl.pallas_call(
        lambda *refs: final_kernel(*refs, long_scale=long_scale),
        name="final",
        out_shape=jax.ShapeDtypeStruct((chans, atoms), bf16),
        in_specs=[whole(pltpu.SMEM)] + [whole()] * 3,
        out_specs=whole(),
        compiler_params=params,
    )(counts, base, longmsg, twice)


def solution(mesh):
    fine = Mesh(mesh.devices.reshape(4, 2, 2, 8, 4), ALL)
    return jax.shard_map(
        local,
        mesh=fine,
        in_specs=(P(None, ALL), P(None, ALL), P(ALL), P(ALL, None), P(), P(), P(), P()),
        out_specs=P(None, ALL),
        check_vma=False,
    )
```

```python
import math

import jax
import jax.numpy as jnp
import numpy as np
from jax import lax
from jax.experimental import pallas as pl
from jax.experimental.pallas import tpu as pltpu
from jax.sharding import Mesh, PartitionSpec as P

box_length = 216.0
pair_scale = 12.5
short_gain = 0.5
long_gain = 16.0
feature_top = 6.0
feature_steps = 32767.0
first_in = 59
first_out = 63
first_near = 4
vmem_limit = 48 * 1024 * 1024

ALL = ("x", "zh", "core", "y", "zl")
DOM = ("x", "zh", "core")
NEAR = ("x", "core")
FAR = ("zh", "y", "zl")

f32 = jnp.float32
bf16 = jnp.bfloat16


def fit_cos(degree):
    nodes = np.cos(np.pi * (np.arange(64) + 0.5) / 64)
    w = 0.125 * (nodes + 1.0)
    cheb = np.polynomial.chebyshev.Chebyshev.fit(w, np.cos(2 * np.pi * np.sqrt(w)), degree, domain=[0.0, 0.25])
    return [float(c) for c in cheb.convert(kind=np.polynomial.Polynomial).coef]


COS_POLY = fit_cos(6)


def turn_cos(v):
    r = v - jnp.floor(v + 0.5)
    w = r * r
    acc = w * COS_POLY[-1] + COS_POLY[-2]
    for c in COS_POLY[-3::-1]:
        acc = acc * w + c
    return acc


def table(turns, kind):
    row = lax.broadcasted_iota(jnp.int32, (8 if kind == "y" else 24, 1), 0)
    if kind == "x":
        freq = 4 * (row >> 3) + (row & 3) + 1
        sine = (row & 4) != 0
    elif kind == "z":
        freq = 2 * (row >> 2) + (row & 1) + 1
        sine = (row & 2) != 0
    else:
        freq = jnp.where(row < 2, 5, jnp.where(row < 4, 10, jnp.where(row < 6, 1, 2)))
        sine = (row & 1) != 0
    return turn_cos(freq.astype(f32) * turns - jnp.where(sine, 0.25, 0.0))


def first_rows(rows):
    sub = lax.broadcasted_iota(jnp.int32, rows.shape, 0)
    return jnp.where(sub < 4, rows, jnp.where(sub == 4, 1.0, 0.0))


def wide_rows(xtab, ytab):
    groups = []
    for g in range(3):
        groups += [xtab[8 * g : 8 * g + 8] * ytab[f : f + 1] for f in range(4)]
    groups += [xtab[8 * g : 8 * g + 8] for g in range(3)]
    return groups + [first_rows(ytab)]


def tall_rows(ztab, ytab):
    sub = lax.broadcasted_iota(jnp.int32, ytab.shape, 0)
    groups = []
    for b in range(2):
        wave = jnp.where(sub < 4, ytab[4 + 2 * b : 5 + 2 * b], ytab[5 + 2 * b : 6 + 2 * b])
        for h in range(6):
            four = ztab[4 * h : 4 * h + 4]
            groups.append(jnp.concatenate([four, four], axis=0) * wave)
    groups += [ztab[8 * g : 8 * g + 8] for g in range(3)]
    return groups + [first_rows(jnp.concatenate([ytab[4:8], ytab[0:4]], axis=0))]


def store_wide(xturns, ytab, e_ref, at):
    groups = wide_rows(table(xturns, "x"), ytab)
    for n in range(0, 16, 2):
        two = jnp.concatenate(groups[n : n + 2], axis=0)
        high = two.astype(bf16)
        e_ref[8 * n : 8 * n + 16, at] = high
        e_ref[128 + 8 * n : 128 + 8 * n + 16, at] = (two - high.astype(f32)).astype(bf16)


def wide_code(lane):
    group, low = lane >> 3, lane & 7
    p = jnp.where(group < 12, 4 * (group >> 2), 4 * (group - 12)) + (low & 3) + 1
    p = jnp.where(group < 15, p, 0)
    a = jnp.where(group < 12, 1 + ((group >> 1) & 1), 0)
    a = jnp.where((group == 15) & (low < 4), 1 + (low >> 1), a)
    return p, a, lane < 125


def wide_masks(lane):
    group, low = lane >> 3, lane & 7
    m_x = jnp.where(group < 15, 4, 0)
    m_a = jnp.where(group < 12, 8, jnp.where((group == 15) & (low < 4), 1, 0))
    s_x = jnp.where((low & 4) != 0, 1.0, -1.0)
    s_a = jnp.where(jnp.where(group < 12, group & 1, low & 1) != 0, 1.0, -1.0)
    return m_x, m_a, s_x, s_a


def tall_code(group, sub):
    mixed, plain = group < 12, group < 15
    r = jnp.where(mixed, 2 * (group % 6) + (sub & 1) + 1, 4 * (group - 12) + 2 * (sub >> 2) + (sub & 1) + 1)
    r = jnp.where(plain, r, 0)
    b = jnp.where(mixed, 1 + group // 6, jnp.where(plain, 0, jnp.where(sub < 4, 1 + (sub >> 1), 0)))
    return b, r, plain | (sub < 5)


def tall_masks(group, sub):
    mixed, plain = group < 12, group < 15
    m_b = jnp.where(mixed, 4, jnp.where(plain, 0, jnp.where(sub < 4, 1, 0)))
    m_z = jnp.where(plain, 2 + 0 * sub, 0)
    s_b = jnp.where(jnp.where(mixed, sub & 4, sub & 1) != 0, 1.0, -1.0)
    s_z = jnp.where((sub & 2) != 0, 1.0, -1.0)
    return m_b, m_z, s_b, s_z


def valid_row(count_ref, atoms):
    slot = lax.broadcasted_iota(jnp.int32, (1, atoms), 1)
    return (slot < count_ref[0]).astype(f32)


def prep_kernel(count_ref, pos_hbm, feat_hbm, pay_ref, pos_ref, feat_ref, sems):
    copies = [
        pltpu.make_async_copy(feat_hbm, feat_ref, sems.at[0]),
        pltpu.make_async_copy(pos_hbm, pos_ref, sems.at[1]),
    ]
    for copy in copies:
        copy.start()
    for copy in copies:
        copy.wait()
    atoms = pos_ref.shape[1]
    masked = feat_ref[...].astype(f32) * valid_row(count_ref, atoms)
    level = jnp.floor(masked * (feature_steps / feature_top) + 0.5).astype(jnp.int32)
    below = jnp.concatenate([level[2:], level[:2]], axis=0)
    words = (level << 16) | (below & 0xFFFF)
    x, y, z = (
        jnp.clip(jnp.floor(pos_ref[i : i + 1, :] * (2.0**bits / box_length) + 0.5).astype(jnp.int32), 0, 2**bits - 1)
        for i, bits in enumerate((21, 21, 22))
    )
    place = jnp.concatenate([(x << 11) | (y >> 10), ((y & 1023) << 22) | z], axis=0)
    for g in range(pay_ref.shape[0]):
        pay_ref[g] = jnp.concatenate([words[4 * g : 4 * g + 2], place], axis=0)


def unpack_turns(in_ref, turns_ref):
    first, second = in_ref[:, 2, :], in_ref[:, 3, :]
    turns_ref[0] = lax.shift_right_logical(first, 11).astype(f32) * 2.0**-21
    turns_ref[1] = (((first & 2047) << 10) | lax.shift_right_logical(second, 22)).astype(f32) * 2.0**-21
    turns_ref[2] = (second & (2**22 - 1)).astype(f32) * 2.0**-22


def faces_kernel(count_ref, core_ref, pos_ref, feat_ref, idx_ref, after_ref, flip_ref, step_ref):
    del after_ref
    atoms = pos_ref.shape[1]
    ghost = idx_ref.shape[1] // 2
    masked = feat_ref[...].astype(f32) * valid_row(count_ref, atoms)
    tail = jnp.concatenate([pos_ref[...], jnp.zeros((1, atoms), f32)], axis=0)
    hi = tail.astype(bf16).astype(f32)
    mid = (tail - hi).astype(bf16).astype(f32)
    lo = (tail - hi) - mid
    parts = jnp.concatenate([masked, hi, mid, lo, jnp.zeros((4, atoms), f32)], axis=0).astype(bf16)
    half = 2 * ghost
    row = lax.broadcasted_iota(jnp.int32, (half, ghost), 0)
    faces = []
    for n in range(2):
        want = idx_ref[0:1, n * ghost : (n + 1) * ghost] - n * half
        pick = (row == want).astype(f32).astype(bf16)
        got = jnp.dot(parts[:, n * half : (n + 1) * half], pick, preferred_element_type=f32)
        place = (got[32:36] + got[36:40]) + got[40:44]
        faces.append(jnp.concatenate([got[0:32], place, jnp.zeros((4, ghost), f32)], axis=0))
    first = core_ref[0] == 0
    flip_ref[...] = jnp.where(first, faces[1], faces[0])
    step_ref[...] = jnp.where(first, faces[0], faces[1])


def factor_kernel(in_ref, out_ref, e_ref, m_ref, turns_ref, line_ref):
    blocks, _, atoms = in_ref.shape
    unpack_turns(in_ref, turns_ref)
    for i in range(2):
        word = in_ref[:, i, :]
        line_ref[i] = (word >> 16).astype(f32) * (feature_top / feature_steps)
        line_ref[2 + i] = ((word << 16) >> 16).astype(f32) * (feature_top / feature_steps)
    total = None
    for k in range(blocks):
        cols = slice(k * atoms, (k + 1) * atoms)
        ytab = table(turns_ref[1, k : k + 1, :], "y")
        store_wide(turns_ref[0, k : k + 1, :], ytab, e_ref, cols)
        groups = tall_rows(table(turns_ref[2, k : k + 1, :], "z"), ytab)
        for c in range(4):
            line = line_ref[c, k : k + 1, :]
            for n in range(0, 16, 2):
                at = 128 * c + 8 * n
                m_ref[at : at + 16, cols] = jnp.concatenate([line * groups[n], line * groups[n + 1]], axis=0).astype(bf16)
        if k % 2:
            cols = slice((k - 1) * atoms, (k + 1) * atoms)
            dims = (((1,), (1,)), ((), ()))
            term = lax.dot_general(m_ref[:, cols], e_ref[:, cols], dims, preferred_element_type=f32)
            total = term if total is None else total + term
    out_ref[...] = (total[:, 0:128] + total[:, 128:256]).astype(bf16)


def coef_kernel(where_ref, kvec_ref, screen_ref, after_ref, out_ref):
    del after_ref
    owner = where_ref[0]
    group = owner % 16
    chan = 4 * where_ref[1] + owner // 16

    p_c, a_c, used_c = wide_code(lax.broadcasted_iota(jnp.int32, (128, 1), 0))
    code_c = jnp.where(used_c, 4 * p_c + a_c, -1)
    b_r, r_r, used_r = tall_code(group, lax.broadcasted_iota(jnp.int32, (8, 1), 0))
    code_r = jnp.where(used_r, 4 * r_r + b_r, -1)
    width = 1024
    counts = jnp.zeros((64, 128), f32)
    for n in range(kvec_ref.shape[1] // width):
        at = slice(n * width, (n + 1) * width)
        kx, ky, kz = kvec_ref[0:1, at], kvec_ref[1:2, at], kvec_ref[2:3, at]
        size = jnp.abs(ky)
        turn = jnp.where(ky < 0, -1, 1)
        ka = jnp.where(size >= 8, 2, jnp.where(size >= 3, 1, 0))
        kb = turn * (size - 5 * ka)
        wide = jnp.where(code_c == 4 * jnp.abs(kx) + ka, 1.0, 0.0).astype(bf16)
        hit = jnp.where(code_r == 4 * jnp.abs(kz) + jnp.abs(kb), 1.0, 0.0)
        sx, sa, sb, sz = (jnp.clip(k, -1, 1).astype(f32) for k in (kx, turn * ka, kb, kz))
        signs = [sx * sa, sx * sb, sx * sz, sa * sb, sa * sz, sb * sz, (sx * sa) * (sb * sz)]
        lines = jnp.concatenate([hit] + [hit * sign for sign in signs], axis=0).astype(bf16)
        counts = counts + lax.dot_general(lines, wide, (((1,), (1,)), ((), ())), preferred_element_type=f32)
    n_0, n_xa, n_xb, n_xz, n_ab, n_az, n_bz, n_all = (counts[8 * v : 8 * v + 8] for v in range(8))

    lane = lax.broadcasted_iota(jnp.int32, (8, 128), 1)
    sub = lax.broadcasted_iota(jnp.int32, (8, 128), 0)
    p, a, used_l = wide_code(lane)
    b, r, used_s = tall_code(group, sub)
    _, _, s_x, s_a = wide_masks(lane)
    _, _, s_b, s_z = tall_masks(group, sub)
    unit = 2.0 * math.pi / box_length
    screen = unit * screen_ref[pl.ds(chan, 1), :]
    screen = screen * screen

    def filt(q):
        return 1.0 / (1.0 + (p * p + q * q + r * r).astype(f32) * screen)

    like, unlike = filt(5 * a + b), filt(5 * a - b)
    used = used_l & used_s
    mean = jnp.where(used, 0.5 * (like + unlike), 0.0)
    half = jnp.where(used, 0.5 * (like - unlike), 0.0)
    out_ref[0] = mean * n_0 + half * n_ab
    out_ref[1] = -(s_x * s_a) * (mean * n_xa + half * n_xb)
    out_ref[2] = -(s_x * s_b) * (mean * n_xb + half * n_xa)
    out_ref[3] = -(s_x * s_z) * (mean * n_xz + half * n_all)
    out_ref[4] = -(s_a * s_b) * (mean * n_ab + half * n_0)
    out_ref[5] = -(s_a * s_z) * (mean * n_az + half * n_bz)
    out_ref[6] = -(s_b * s_z) * (mean * n_bz + half * n_az)
    out_ref[7] = (s_x * s_a) * (s_b * s_z) * (mean * n_all + half * n_xz)


def owner_kernel(where_ref, part_ref, coef_ref, step_ref, g1_ref, out_ref, step_out):
    del g1_ref
    step_out[...] = step_ref[...]
    group = where_ref[0] % 16
    totals = [part_ref[16 * n : 16 * n + 16, :].astype(f32) for n in range(4)]
    for n in range(4, part_ref.shape[0] // 16):
        totals[n % 4] = totals[n % 4] + part_ref[16 * n : 16 * n + 16, :].astype(f32)
    total = (totals[0] + totals[1]) + (totals[2] + totals[3])
    total = total[0:8] + total[8:16]
    lane = lax.broadcasted_iota(jnp.int32, (8, 128), 1)
    sub = lax.broadcasted_iota(jnp.int32, (8, 128), 0)
    m_x, m_a, _, _ = wide_masks(lane)
    m_b, m_z, _, _ = tall_masks(group, sub)

    def lanes(value, mask):
        return jnp.take_along_axis(value, lane ^ mask, axis=1)

    def rows(value, mask):
        return jnp.take_along_axis(value, sub ^ mask, axis=0)

    t_x, t_a, t_xa = lanes(total, m_x), lanes(total, m_a), lanes(total, m_x ^ m_a)
    terms = [
        total,
        t_xa,
        rows(t_x, m_b),
        rows(t_x, m_z),
        rows(t_a, m_b),
        rows(t_a, m_z),
        rows(total, m_b ^ m_z),
        rows(t_xa, m_b ^ m_z),
    ]
    done = coef_ref[0] * terms[0]
    for n in range(1, 8):
        done = done + coef_ref[n] * terms[n]
    twice = jnp.concatenate([done, done], axis=0).astype(bf16)
    for n in range(out_ref.shape[0] // 16):
        out_ref[16 * n : 16 * n + 16, :] = twice


def field_blocks(first, filt_ref, in_ref, out_ref, e_ref, g_ref, turns_ref):
    unpack_turns(in_ref, turns_ref)
    rows = filt_ref.shape[0]
    late = 8 * (first_out - first_in) % rows
    for at in (0, 128):
        g_ref[late:rows, at : at + 128] = filt_ref[0 : rows - late, :]
        if late:
            g_ref[0:late, at : at + 128] = filt_ref[rows - late : rows, :]
    atoms = out_ref.shape[2]
    for k in range(first, out_ref.shape[0]):
        cols = slice((k - first) * atoms, (k - first + 1) * atoms)
        ytab = table(turns_ref[1, k : k + 1, :], "y")
        store_wide(turns_ref[0, k : k + 1, :], ytab, e_ref, cols)
        groups = tall_rows(table(turns_ref[2, k : k + 1, :], "z"), ytab)
        term = jnp.dot(g_ref[...], e_ref[:, cols], preferred_element_type=f32)
        lines = []
        for c in range(4):
            acc = term[128 * c : 128 * c + 8] * groups[0]
            for n in range(1, 16):
                acc = acc + term[128 * c + 8 * n : 128 * c + 8 * n + 8] * groups[n]
            lines.append(jnp.sum(acc, axis=0, keepdims=True))
        out_ref[k] = jnp.concatenate(lines, axis=0)


def field_kernel(filt_ref, in_ref, own_ref, out_ref, e_ref, g_ref, turns_ref):
    del own_ref
    field_blocks(0, filt_ref, in_ref, out_ref, e_ref, g_ref, turns_ref)


def rest_kernel(filt_ref, in_ref, part_ref, g2_ref, out_ref, e_ref, g_ref, turns_ref):
    del g2_ref
    done = part_ref.shape[0]
    out_ref[0:done] = part_ref[...]
    field_blocks(done, filt_ref, in_ref, out_ref, e_ref, g_ref, turns_ref)


shrink = math.sqrt(math.log2(math.e) / pair_scale)


def pairs(cols, rows, wrap):
    box = box_length * shrink
    dx = cols[:, 0:1] - rows[0:1]
    if wrap:
        dx = jnp.abs(dx)
        dx = jnp.minimum(dx, box - dx)
    dy = cols[:, 1:2] - rows[1:2]
    dz = jnp.abs(cols[:, 2:3] - rows[2:3])
    dz = jnp.minimum(dz, box - dz)
    return jnp.exp2(-(dx * dx + dy * dy + dz * dz)).astype(bf16)


def own_kernel(count_ref, pos_ref, feat_ref, after_ref, out_ref):
    del after_ref
    atoms = pos_ref.shape[1]
    masked = (feat_ref[...].astype(f32) * valid_row(count_ref, atoms)).astype(bf16)
    rows = pos_ref[...] * shrink
    rows8 = jnp.concatenate([rows, jnp.zeros((5, atoms), f32)], axis=0)
    step = 256
    total = None
    for n in range(atoms // step):
        at = slice(n * step, (n + 1) * step)
        term = jnp.dot(masked[:, at], pairs(jnp.transpose(rows8[:, at]), rows, False), preferred_element_type=f32)
        total = term if total is None else total + term
    out_ref[...] = total


def short_kernel(pos_ref, feat_ref, g1_ref, g2_ref, own_ref, lw_ref, sw_ref, after_ref, base_ref, twice_ref):
    del after_ref
    ghost = jnp.concatenate([g1_ref[...], g2_ref[...]], axis=1)
    near_by = pairs(jnp.transpose(ghost[32:40] * shrink), pos_ref[...] * shrink, True)
    short = own_ref[...] + jnp.dot(ghost[0:32].astype(bf16), near_by, preferred_element_type=f32)
    mixed = jnp.dot(stacked(sw_ref[...]), split(short), preferred_element_type=f32)
    base_ref[...] = feat_ref[...].astype(f32) + short_gain * mixed
    twice_ref[...] = stacked(lw_ref[...])


def stacked(weight):
    turned = jnp.transpose(weight.astype(f32))
    return jnp.concatenate([turned, turned], axis=1).astype(bf16)


def split(value):
    high = value.astype(bf16)
    low = (value - high.astype(f32)).astype(bf16)
    return jnp.concatenate([high, low], axis=0)


def final_kernel(count_ref, base_ref, long_ref, twice_ref, out_ref, *, long_scale):
    mixed = jnp.dot(twice_ref[...], split(long_ref[...]), preferred_element_type=f32)
    total = base_ref[...] + long_scale * mixed
    out_ref[...] = (total * valid_row(count_ref, total.shape[1])).astype(bf16)


def swap_parts(parts, axis, first):
    count = parts.shape[0]
    order = [[(n + first) % count for n in range(count)]]
    return lax.all_to_all(parts, axis, 0, 0, axis_index_groups=order, tiled=True)


def whole(memory=pltpu.VMEM):
    return pl.BlockSpec(memory_space=memory)


def local(positions, features, counts, ghost_index, kvec, screen_len, long_weight, short_weight):
    chans, atoms = features.shape
    total_vec = kvec.shape[1]
    ghost = ghost_index.shape[1] // 2
    near = lax.axis_size(NEAR)
    far = lax.axis_size(FAR)
    params = pltpu.CompilerParams(vmem_limit_bytes=vmem_limit)

    payload = pl.pallas_call(
        prep_kernel,
        name="prep",
        out_shape=jax.ShapeDtypeStruct((near, 4, atoms), jnp.int32),
        in_specs=[whole(pltpu.SMEM), whole(pl.ANY), whole(pl.ANY)],
        out_specs=whole(),
        scratch_shapes=[
            pltpu.VMEM(positions.shape, f32),
            pltpu.VMEM(features.shape, bf16),
            pltpu.SemaphoreType.DMA((2,)),
        ],
    )(counts, positions, features)
    gathered = swap_parts(payload, NEAR, first_near)

    rows = jax.ShapeDtypeStruct((8 * far, 128), bf16)

    def exchange(value, first):
        parts = value.reshape(far, 8, 128)
        return swap_parts(parts, FAR, first).reshape(8 * far, 128)

    partial = pl.pallas_call(
        factor_kernel,
        name="factor",
        out_shape=rows,
        in_specs=[whole()],
        out_specs=whole(),
        scratch_shapes=[
            pltpu.VMEM((256, near * atoms), bf16),
            pltpu.VMEM((512, near * atoms), bf16),
            pltpu.VMEM((3, near, atoms), f32),
            pltpu.VMEM((4, near, atoms), f32),
        ],
        compiler_params=params,
    )(gathered)
    spread = exchange(partial, first_in)

    owner = (lax.axis_index(FAR) + far - first_in) % far
    share = (lax.axis_index(NEAR) + near - first_near) % near
    place = jnp.stack([owner, share]).astype(jnp.int32)
    screens = jnp.broadcast_to(screen_len[:, None], (chans, 128))
    coef = pl.pallas_call(
        coef_kernel,
        name="coef",
        out_shape=jax.ShapeDtypeStruct((8, 8, 128), f32),
        in_specs=[whole(pltpu.SMEM), whole(), whole(), whole(pl.ANY)],
        out_specs=whole(),
        compiler_params=params,
        cost_estimate=pl.CostEstimate(flops=2 * 64 * 256 * total_vec, bytes_accessed=8 * total_vec, transcendentals=0),
    )(place, kvec, screens, partial)
    core = lax.axis_index("core").reshape(1).astype(jnp.int32)
    face = jax.ShapeDtypeStruct((chans + 8, ghost), f32)
    flip_face, step_face = pl.pallas_call(
        faces_kernel,
        name="faces",
        out_shape=[face, face],
        in_specs=[whole(pltpu.SMEM), whole(pltpu.SMEM), whole(), whole(), whole(), whole(pl.ANY)],
        out_specs=[whole(), whole()],
        compiler_params=params,
    )(counts, core, positions, features, ghost_index, partial)
    n_dom = lax.axis_size(DOM)
    flip = [(d, d ^ 1) for d in range(n_dom)]
    step = [(d, (d + 1) % n_dom if d % 2 else (d - 1) % n_dom) for d in range(n_dom)]
    ghosts_1 = lax.ppermute(flip_face, DOM, flip)
    filtered, step_face = pl.pallas_call(
        owner_kernel,
        name="owner",
        out_shape=[rows, face],
        in_specs=[whole(pltpu.SMEM)] + [whole()] * 3 + [whole(pl.ANY)],
        out_specs=[whole()] * 2,
        compiler_params=params,
    )(place, spread, coef, step_face, ghosts_1)
    everywhere = exchange(filtered, first_out)
    ghosts_2 = lax.ppermute(step_face, DOM, step)
    own = pl.pallas_call(
        own_kernel,
        name="own",
        out_shape=jax.ShapeDtypeStruct((chans, atoms), f32),
        in_specs=[whole(pltpu.SMEM), whole(), whole(), whole(pl.ANY)],
        out_specs=whole(),
        compiler_params=params,
    )(counts, positions, features, filtered)
    early = near * 7 // 8
    field_scratch = [
        pltpu.VMEM((256, max(early, near - early) * atoms), bf16),
        pltpu.VMEM((512, 256), bf16),
        pltpu.VMEM((3, near, atoms), f32),
    ]
    field = pl.pallas_call(
        field_kernel,
        name="field",
        out_shape=jax.ShapeDtypeStruct((early, 4, atoms), f32),
        in_specs=[whole()] * 2 + [whole(pl.ANY)],
        out_specs=whole(),
        scratch_shapes=field_scratch,
        compiler_params=params,
    )(everywhere, gathered, own)
    field = pl.pallas_call(
        rest_kernel,
        name="rest",
        out_shape=jax.ShapeDtypeStruct((near, 4, atoms), f32),
        in_specs=[whole()] * 3 + [whole(pl.ANY)],
        out_specs=whole(),
        scratch_shapes=field_scratch,
        compiler_params=params,
    )(everywhere, gathered, field, ghosts_2)
    base, twice = pl.pallas_call(
        short_kernel,
        name="short",
        out_shape=[jax.ShapeDtypeStruct((chans, atoms), f32), jax.ShapeDtypeStruct((chans, 2 * chans), bf16)],
        in_specs=[whole()] * 7 + [whole(pl.ANY)],
        out_specs=[whole()] * 2,
        compiler_params=params,
        cost_estimate=pl.CostEstimate(flops=2 * 256 * 256 * atoms, bytes_accessed=10 * 32 * atoms, transcendentals=256 * atoms),
    )(positions, features, ghosts_1, ghosts_2, own, long_weight, short_weight, field)
    longmsg = swap_parts(field, NEAR, first_near).reshape(chans, atoms)
    all_atoms = atoms * lax.axis_size(ALL)
    long_scale = long_gain / math.sqrt(total_vec * all_atoms)
    return pl.pallas_call(
        lambda *refs: final_kernel(*refs, long_scale=long_scale),
        name="final",
        out_shape=jax.ShapeDtypeStruct((chans, atoms), bf16),
        in_specs=[whole(pltpu.SMEM)] + [whole()] * 3,
        out_specs=whole(),
        compiler_params=params,
    )(counts, base, longmsg, twice)


def solution(mesh):
    fine = Mesh(mesh.devices.reshape(4, 2, 2, 8, 4), ALL)
    return jax.shard_map(
        local,
        mesh=fine,
        in_specs=(P(None, ALL), P(None, ALL), P(ALL), P(ALL, None), P(), P(), P(), P()),
        out_specs=P(None, ALL),
        check_vma=False,
    )
```

```python
import math

import jax
import jax.numpy as jnp
import numpy as np
from jax import lax
from jax.experimental import pallas as pl
from jax.experimental.pallas import tpu as pltpu
from jax.sharding import Mesh, PartitionSpec as P

box_length = 216.0
pair_scale = 12.5
short_gain = 0.5
long_gain = 16.0
feature_top = 6.0
feature_steps = 32767.0
first_in = 59
first_out = 63
first_near = 4
vmem_limit = 48 * 1024 * 1024

ALL = ("x", "zh", "core", "y", "zl")
DOM = ("x", "zh", "core")
NEAR = ("x", "core")
FAR = ("zh", "y", "zl")

f32 = jnp.float32
bf16 = jnp.bfloat16


def fit_cos(degree):
    nodes = np.cos(np.pi * (np.arange(64) + 0.5) / 64)
    w = 0.125 * (nodes + 1.0)
    cheb = np.polynomial.chebyshev.Chebyshev.fit(w, np.cos(2 * np.pi * np.sqrt(w)), degree, domain=[0.0, 0.25])
    return [float(c) for c in cheb.convert(kind=np.polynomial.Polynomial).coef]


COS_POLY = fit_cos(6)


def turn_cos(v):
    r = v - jnp.floor(v + 0.5)
    w = r * r
    acc = w * COS_POLY[-1] + COS_POLY[-2]
    for c in COS_POLY[-3::-1]:
        acc = acc * w + c
    return acc


def table(turns, kind):
    row = lax.broadcasted_iota(jnp.int32, (8 if kind == "y" else 24, 1), 0)
    if kind == "x":
        freq = 4 * (row >> 3) + (row & 3) + 1
        sine = (row & 4) != 0
    elif kind == "z":
        freq = 2 * (row >> 2) + (row & 1) + 1
        sine = (row & 2) != 0
    else:
        freq = jnp.where(row < 2, 5, jnp.where(row < 4, 10, jnp.where(row < 6, 1, 2)))
        sine = (row & 1) != 0
    return turn_cos(freq.astype(f32) * turns - jnp.where(sine, 0.25, 0.0))


def first_rows(rows):
    sub = lax.broadcasted_iota(jnp.int32, rows.shape, 0)
    return jnp.where(sub < 4, rows, jnp.where(sub == 4, 1.0, 0.0))


def wide_rows(xtab, ytab):
    groups = []
    for g in range(3):
        groups += [xtab[8 * g : 8 * g + 8] * ytab[f : f + 1] for f in range(4)]
    groups += [xtab[8 * g : 8 * g + 8] for g in range(3)]
    return groups + [first_rows(ytab)]


def tall_rows(ztab, ytab):
    sub = lax.broadcasted_iota(jnp.int32, ytab.shape, 0)
    groups = []
    for b in range(2):
        wave = jnp.where(sub < 4, ytab[4 + 2 * b : 5 + 2 * b], ytab[5 + 2 * b : 6 + 2 * b])
        for h in range(6):
            four = ztab[4 * h : 4 * h + 4]
            groups.append(jnp.concatenate([four, four], axis=0) * wave)
    groups += [ztab[8 * g : 8 * g + 8] for g in range(3)]
    return groups + [first_rows(jnp.concatenate([ytab[4:8], ytab[0:4]], axis=0))]


def store_wide(xturns, ytab, e_ref, at):
    groups = wide_rows(table(xturns, "x"), ytab)
    for n in range(0, 16, 2):
        two = jnp.concatenate(groups[n : n + 2], axis=0)
        high = two.astype(bf16)
        e_ref[8 * n : 8 * n + 16, at] = high
        e_ref[128 + 8 * n : 128 + 8 * n + 16, at] = (two - high.astype(f32)).astype(bf16)


def wide_code(lane):
    group, low = lane >> 3, lane & 7
    p = jnp.where(group < 12, 4 * (group >> 2), 4 * (group - 12)) + (low & 3) + 1
    p = jnp.where(group < 15, p, 0)
    a = jnp.where(group < 12, 1 + ((group >> 1) & 1), 0)
    a = jnp.where((group == 15) & (low < 4), 1 + (low >> 1), a)
    return p, a, lane < 125


def wide_masks(lane):
    group, low = lane >> 3, lane & 7
    m_x = jnp.where(group < 15, 4, 0)
    m_a = jnp.where(group < 12, 8, jnp.where((group == 15) & (low < 4), 1, 0))
    s_x = jnp.where((low & 4) != 0, 1.0, -1.0)
    s_a = jnp.where(jnp.where(group < 12, group & 1, low & 1) != 0, 1.0, -1.0)
    return m_x, m_a, s_x, s_a


def tall_code(group, sub):
    mixed, plain = group < 12, group < 15
    r = jnp.where(mixed, 2 * (group % 6) + (sub & 1) + 1, 4 * (group - 12) + 2 * (sub >> 2) + (sub & 1) + 1)
    r = jnp.where(plain, r, 0)
    b = jnp.where(mixed, 1 + group // 6, jnp.where(plain, 0, jnp.where(sub < 4, 1 + (sub >> 1), 0)))
    return b, r, plain | (sub < 5)


def tall_masks(group, sub):
    mixed, plain = group < 12, group < 15
    m_b = jnp.where(mixed, 4, jnp.where(plain, 0, jnp.where(sub < 4, 1, 0)))
    m_z = jnp.where(plain, 2 + 0 * sub, 0)
    s_b = jnp.where(jnp.where(mixed, sub & 4, sub & 1) != 0, 1.0, -1.0)
    s_z = jnp.where((sub & 2) != 0, 1.0, -1.0)
    return m_b, m_z, s_b, s_z


def valid_row(count_ref, atoms):
    slot = lax.broadcasted_iota(jnp.int32, (1, atoms), 1)
    return (slot < count_ref[0]).astype(f32)


def prep_kernel(count_ref, pos_hbm, feat_hbm, pay_ref, pos_ref, feat_ref, sems):
    copies = [
        pltpu.make_async_copy(feat_hbm, feat_ref, sems.at[0]),
        pltpu.make_async_copy(pos_hbm, pos_ref, sems.at[1]),
    ]
    for copy in copies:
        copy.start()
    for copy in copies:
        copy.wait()
    atoms = pos_ref.shape[1]
    masked = feat_ref[...].astype(f32) * valid_row(count_ref, atoms)
    level = jnp.floor(masked * (feature_steps / feature_top) + 0.5).astype(jnp.int32)
    below = jnp.concatenate([level[2:], level[:2]], axis=0)
    words = (level << 16) | (below & 0xFFFF)
    x, y, z = (
        jnp.clip(jnp.floor(pos_ref[i : i + 1, :] * (2.0**bits / box_length) + 0.5).astype(jnp.int32), 0, 2**bits - 1)
        for i, bits in enumerate((21, 21, 22))
    )
    place = jnp.concatenate([(x << 11) | (y >> 10), ((y & 1023) << 22) | z], axis=0)
    for g in range(pay_ref.shape[0]):
        pay_ref[g] = jnp.concatenate([words[4 * g : 4 * g + 2], place], axis=0)


def unpack_turns(in_ref, turns_ref):
    first, second = in_ref[:, 2, :], in_ref[:, 3, :]
    turns_ref[0] = lax.shift_right_logical(first, 11).astype(f32) * 2.0**-21
    turns_ref[1] = (((first & 2047) << 10) | lax.shift_right_logical(second, 22)).astype(f32) * 2.0**-21
    turns_ref[2] = (second & (2**22 - 1)).astype(f32) * 2.0**-22


def faces_kernel(count_ref, core_ref, pos_ref, feat_ref, idx_ref, after_ref, flip_ref, step_ref):
    del after_ref
    atoms = pos_ref.shape[1]
    ghost = idx_ref.shape[1] // 2
    masked = feat_ref[...].astype(f32) * valid_row(count_ref, atoms)
    tail = jnp.concatenate([pos_ref[...], jnp.zeros((1, atoms), f32)], axis=0)
    hi = tail.astype(bf16).astype(f32)
    mid = (tail - hi).astype(bf16).astype(f32)
    lo = (tail - hi) - mid
    parts = jnp.concatenate([masked, hi, mid, lo, jnp.zeros((4, atoms), f32)], axis=0).astype(bf16)
    half = 2 * ghost
    row = lax.broadcasted_iota(jnp.int32, (half, ghost), 0)
    faces = []
    for n in range(2):
        want = idx_ref[0:1, n * ghost : (n + 1) * ghost] - n * half
        pick = (row == want).astype(f32).astype(bf16)
        got = jnp.dot(parts[:, n * half : (n + 1) * half], pick, preferred_element_type=f32)
        place = (got[32:36] + got[36:40]) + got[40:44]
        faces.append(jnp.concatenate([got[0:32], place, jnp.zeros((4, ghost), f32)], axis=0))
    first = core_ref[0] == 0
    flip_ref[...] = jnp.where(first, faces[1], faces[0])
    step_ref[...] = jnp.where(first, faces[0], faces[1])


def factor_kernel(in_ref, out_ref, e_ref, m_ref, turns_ref, line_ref):
    blocks, _, atoms = in_ref.shape
    unpack_turns(in_ref, turns_ref)
    for i in range(2):
        word = in_ref[:, i, :]
        line_ref[i] = (word >> 16).astype(f32) * (feature_top / feature_steps)
        line_ref[2 + i] = ((word << 16) >> 16).astype(f32) * (feature_top / feature_steps)
    total = None
    for k in range(blocks):
        cols = slice(k * atoms, (k + 1) * atoms)
        ytab = table(turns_ref[1, k : k + 1, :], "y")
        store_wide(turns_ref[0, k : k + 1, :], ytab, e_ref, cols)
        groups = tall_rows(table(turns_ref[2, k : k + 1, :], "z"), ytab)
        for c in range(4):
            line = line_ref[c, k : k + 1, :]
            for n in range(0, 16, 2):
                at = 128 * c + 8 * n
                m_ref[at : at + 16, cols] = jnp.concatenate([line * groups[n], line * groups[n + 1]], axis=0).astype(bf16)
        if k % 2:
            cols = slice((k - 1) * atoms, (k + 1) * atoms)
            dims = (((1,), (1,)), ((), ()))
            term = lax.dot_general(m_ref[:, cols], e_ref[:, cols], dims, preferred_element_type=f32)
            total = term if total is None else total + term
    out_ref[...] = (total[:, 0:128] + total[:, 128:256]).astype(bf16)


def coef_kernel(where_ref, kvec_ref, screen_ref, after_ref, out_ref):
    del after_ref
    owner = where_ref[0]
    group = owner % 16
    chan = 4 * where_ref[1] + owner // 16

    p_c, a_c, used_c = wide_code(lax.broadcasted_iota(jnp.int32, (128, 1), 0))
    code_c = jnp.where(used_c, 4 * p_c + a_c, -1)
    b_r, r_r, used_r = tall_code(group, lax.broadcasted_iota(jnp.int32, (8, 1), 0))
    code_r = jnp.where(used_r, 4 * r_r + b_r, -1)
    width = 1024
    counts = jnp.zeros((64, 128), f32)
    for n in range(kvec_ref.shape[1] // width):
        at = slice(n * width, (n + 1) * width)
        kx, ky, kz = kvec_ref[0:1, at], kvec_ref[1:2, at], kvec_ref[2:3, at]
        size = jnp.abs(ky)
        turn = jnp.where(ky < 0, -1, 1)
        ka = jnp.where(size >= 8, 2, jnp.where(size >= 3, 1, 0))
        kb = turn * (size - 5 * ka)
        wide = jnp.where(code_c == 4 * jnp.abs(kx) + ka, 1.0, 0.0).astype(bf16)
        hit = jnp.where(code_r == 4 * jnp.abs(kz) + jnp.abs(kb), 1.0, 0.0)
        sx, sa, sb, sz = (jnp.clip(k, -1, 1).astype(f32) for k in (kx, turn * ka, kb, kz))
        signs = [sx * sa, sx * sb, sx * sz, sa * sb, sa * sz, sb * sz, (sx * sa) * (sb * sz)]
        lines = jnp.concatenate([hit] + [hit * sign for sign in signs], axis=0).astype(bf16)
        counts = counts + lax.dot_general(lines, wide, (((1,), (1,)), ((), ())), preferred_element_type=f32)
    n_0, n_xa, n_xb, n_xz, n_ab, n_az, n_bz, n_all = (counts[8 * v : 8 * v + 8] for v in range(8))

    lane = lax.broadcasted_iota(jnp.int32, (8, 128), 1)
    sub = lax.broadcasted_iota(jnp.int32, (8, 128), 0)
    p, a, used_l = wide_code(lane)
    b, r, used_s = tall_code(group, sub)
    _, _, s_x, s_a = wide_masks(lane)
    _, _, s_b, s_z = tall_masks(group, sub)
    unit = 2.0 * math.pi / box_length
    screen = unit * screen_ref[pl.ds(chan, 1), :]
    screen = screen * screen

    def filt(q):
        return 1.0 / (1.0 + (p * p + q * q + r * r).astype(f32) * screen)

    like, unlike = filt(5 * a + b), filt(5 * a - b)
    used = used_l & used_s
    mean = jnp.where(used, 0.5 * (like + unlike), 0.0)
    half = jnp.where(used, 0.5 * (like - unlike), 0.0)
    out_ref[0] = mean * n_0 + half * n_ab
    out_ref[1] = -(s_x * s_a) * (mean * n_xa + half * n_xb)
    out_ref[2] = -(s_x * s_b) * (mean * n_xb + half * n_xa)
    out_ref[3] = -(s_x * s_z) * (mean * n_xz + half * n_all)
    out_ref[4] = -(s_a * s_b) * (mean * n_ab + half * n_0)
    out_ref[5] = -(s_a * s_z) * (mean * n_az + half * n_bz)
    out_ref[6] = -(s_b * s_z) * (mean * n_bz + half * n_az)
    out_ref[7] = (s_x * s_a) * (s_b * s_z) * (mean * n_all + half * n_xz)


def owner_kernel(where_ref, part_ref, coef_ref, step_ref, g1_ref, out_ref, step_out):
    del g1_ref
    step_out[...] = step_ref[...]
    group = where_ref[0] % 16
    totals = [part_ref[16 * n : 16 * n + 16, :].astype(f32) for n in range(4)]
    for n in range(4, part_ref.shape[0] // 16):
        totals[n % 4] = totals[n % 4] + part_ref[16 * n : 16 * n + 16, :].astype(f32)
    total = (totals[0] + totals[1]) + (totals[2] + totals[3])
    total = total[0:8] + total[8:16]
    lane = lax.broadcasted_iota(jnp.int32, (8, 128), 1)
    sub = lax.broadcasted_iota(jnp.int32, (8, 128), 0)
    m_x, m_a, _, _ = wide_masks(lane)
    m_b, m_z, _, _ = tall_masks(group, sub)

    def lanes(value, mask):
        return jnp.take_along_axis(value, lane ^ mask, axis=1)

    def rows(value, mask):
        return jnp.take_along_axis(value, sub ^ mask, axis=0)

    t_x, t_a, t_xa = lanes(total, m_x), lanes(total, m_a), lanes(total, m_x ^ m_a)
    terms = [
        total,
        t_xa,
        rows(t_x, m_b),
        rows(t_x, m_z),
        rows(t_a, m_b),
        rows(t_a, m_z),
        rows(total, m_b ^ m_z),
        rows(t_xa, m_b ^ m_z),
    ]
    done = coef_ref[0] * terms[0]
    for n in range(1, 8):
        done = done + coef_ref[n] * terms[n]
    twice = jnp.concatenate([done, done], axis=0).astype(bf16)
    for n in range(out_ref.shape[0] // 16):
        out_ref[16 * n : 16 * n + 16, :] = twice


def field_blocks(first, last, filt_ref, in_ref, e_ref, g_ref, turns_ref):
    unpack_turns(in_ref, turns_ref)
    rows = filt_ref.shape[0]
    late = 8 * (first_out - first_in) % rows
    for at in (0, 128):
        g_ref[late:rows, at : at + 128] = filt_ref[0 : rows - late, :]
        if late:
            g_ref[0:late, at : at + 128] = filt_ref[rows - late : rows, :]
    atoms = in_ref.shape[2]
    found = []
    for k in range(first, last):
        cols = slice((k - first) * atoms, (k - first + 1) * atoms)
        ytab = table(turns_ref[1, k : k + 1, :], "y")
        store_wide(turns_ref[0, k : k + 1, :], ytab, e_ref, cols)
        groups = tall_rows(table(turns_ref[2, k : k + 1, :], "z"), ytab)
        term = jnp.dot(g_ref[...], e_ref[:, cols], preferred_element_type=f32)
        lines = []
        for c in range(4):
            acc = term[128 * c : 128 * c + 8] * groups[0]
            for n in range(1, 16):
                acc = acc + term[128 * c + 8 * n : 128 * c + 8 * n + 8] * groups[n]
            lines.append(jnp.sum(acc, axis=0, keepdims=True))
        found.append(jnp.concatenate(lines, axis=0))
    return found


def field_kernel(filt_ref, in_ref, own_ref, out_ref, e_ref, g_ref, turns_ref):
    del own_ref
    for k, lines in enumerate(field_blocks(0, out_ref.shape[0], filt_ref, in_ref, e_ref, g_ref, turns_ref)):
        out_ref[k] = lines


def rest_kernel(filt_ref, in_ref, part_ref, g2_ref, out_ref, e_ref, g_ref, turns_ref):
    del g2_ref
    done = part_ref.shape[0]
    found = field_blocks(done, in_ref.shape[0], filt_ref, in_ref, e_ref, g_ref, turns_ref)
    out_ref[...] = jnp.concatenate([part_ref[k] for k in range(done)] + found, axis=0).astype(bf16)


shrink = math.sqrt(math.log2(math.e) / pair_scale)


def pairs(cols, rows, wrap):
    box = box_length * shrink
    dx = cols[:, 0:1] - rows[0:1]
    if wrap:
        dx = jnp.abs(dx)
        dx = jnp.minimum(dx, box - dx)
    dy = cols[:, 1:2] - rows[1:2]
    dz = jnp.abs(cols[:, 2:3] - rows[2:3])
    dz = jnp.minimum(dz, box - dz)
    return jnp.exp2(-(dx * dx + dy * dy + dz * dz)).astype(bf16)


def own_kernel(count_ref, pos_ref, feat_ref, after_ref, out_ref):
    del after_ref
    atoms = pos_ref.shape[1]
    masked = (feat_ref[...].astype(f32) * valid_row(count_ref, atoms)).astype(bf16)
    rows = pos_ref[...] * shrink
    rows8 = jnp.concatenate([rows, jnp.zeros((5, atoms), f32)], axis=0)
    step = 256
    total = None
    for n in range(atoms // step):
        at = slice(n * step, (n + 1) * step)
        term = jnp.dot(masked[:, at], pairs(jnp.transpose(rows8[:, at]), rows, False), preferred_element_type=f32)
        total = term if total is None else total + term
    out_ref[...] = total


def short_kernel(pos_ref, feat_ref, g1_ref, g2_ref, own_ref, lw_ref, sw_ref, after_ref, base_ref, twice_ref):
    del after_ref
    ghost = jnp.concatenate([g1_ref[...], g2_ref[...]], axis=1)
    near_by = pairs(jnp.transpose(ghost[32:40] * shrink), pos_ref[...] * shrink, True)
    short = own_ref[...] + jnp.dot(ghost[0:32].astype(bf16), near_by, preferred_element_type=f32)
    mixed = jnp.dot(stacked(sw_ref[...]), split(short), preferred_element_type=f32)
    base_ref[...] = feat_ref[...].astype(f32) + short_gain * mixed
    twice_ref[...] = stacked(lw_ref[...])


def stacked(weight):
    turned = jnp.transpose(weight.astype(f32))
    return jnp.concatenate([turned, turned], axis=1).astype(bf16)


def split(value):
    high = value.astype(bf16)
    low = (value - high.astype(f32)).astype(bf16)
    return jnp.concatenate([high, low], axis=0)


def final_kernel(count_ref, base_ref, long_ref, twice_ref, out_ref, *, long_scale):
    mixed = jnp.dot(twice_ref[...], split(long_ref[...].astype(f32)), preferred_element_type=f32)
    total = base_ref[...] + long_scale * mixed
    out_ref[...] = (total * valid_row(count_ref, total.shape[1])).astype(bf16)


def swap_parts(parts, axis, first):
    count = parts.shape[0]
    order = [[(n + first) % count for n in range(count)]]
    return lax.all_to_all(parts, axis, 0, 0, axis_index_groups=order, tiled=True)


def whole(memory=pltpu.VMEM):
    return pl.BlockSpec(memory_space=memory)


def local(positions, features, counts, ghost_index, kvec, screen_len, long_weight, short_weight):
    chans, atoms = features.shape
    total_vec = kvec.shape[1]
    ghost = ghost_index.shape[1] // 2
    near = lax.axis_size(NEAR)
    far = lax.axis_size(FAR)
    params = pltpu.CompilerParams(vmem_limit_bytes=vmem_limit)

    payload = pl.pallas_call(
        prep_kernel,
        name="prep",
        out_shape=jax.ShapeDtypeStruct((near, 4, atoms), jnp.int32),
        in_specs=[whole(pltpu.SMEM), whole(pl.ANY), whole(pl.ANY)],
        out_specs=whole(),
        scratch_shapes=[
            pltpu.VMEM(positions.shape, f32),
            pltpu.VMEM(features.shape, bf16),
            pltpu.SemaphoreType.DMA((2,)),
        ],
    )(counts, positions, features)
    gathered = swap_parts(payload, NEAR, first_near)

    rows = jax.ShapeDtypeStruct((8 * far, 128), bf16)

    def exchange(value, first):
        parts = value.reshape(far, 8, 128)
        return swap_parts(parts, FAR, first).reshape(8 * far, 128)

    partial = pl.pallas_call(
        factor_kernel,
        name="factor",
        out_shape=rows,
        in_specs=[whole()],
        out_specs=whole(),
        scratch_shapes=[
            pltpu.VMEM((256, near * atoms), bf16),
            pltpu.VMEM((512, near * atoms), bf16),
            pltpu.VMEM((3, near, atoms), f32),
            pltpu.VMEM((4, near, atoms), f32),
        ],
        compiler_params=params,
    )(gathered)
    spread = exchange(partial, first_in)

    owner = (lax.axis_index(FAR) + far - first_in) % far
    share = (lax.axis_index(NEAR) + near - first_near) % near
    place = jnp.stack([owner, share]).astype(jnp.int32)
    screens = jnp.broadcast_to(screen_len[:, None], (chans, 128))
    coef = pl.pallas_call(
        coef_kernel,
        name="coef",
        out_shape=jax.ShapeDtypeStruct((8, 8, 128), f32),
        in_specs=[whole(pltpu.SMEM), whole(), whole(), whole(pl.ANY)],
        out_specs=whole(),
        compiler_params=params,
        cost_estimate=pl.CostEstimate(flops=2 * 64 * 256 * total_vec, bytes_accessed=8 * total_vec, transcendentals=0),
    )(place, kvec, screens, partial)
    core = lax.axis_index("core").reshape(1).astype(jnp.int32)
    face = jax.ShapeDtypeStruct((chans + 8, ghost), f32)
    flip_face, step_face = pl.pallas_call(
        faces_kernel,
        name="faces",
        out_shape=[face, face],
        in_specs=[whole(pltpu.SMEM), whole(pltpu.SMEM), whole(), whole(), whole(), whole(pl.ANY)],
        out_specs=[whole(), whole()],
        compiler_params=params,
    )(counts, core, positions, features, ghost_index, partial)
    n_dom = lax.axis_size(DOM)
    flip = [(d, d ^ 1) for d in range(n_dom)]
    step = [(d, (d + 1) % n_dom if d % 2 else (d - 1) % n_dom) for d in range(n_dom)]
    ghosts_1 = lax.ppermute(flip_face, DOM, flip)
    filtered, step_face = pl.pallas_call(
        owner_kernel,
        name="owner",
        out_shape=[rows, face],
        in_specs=[whole(pltpu.SMEM)] + [whole()] * 3 + [whole(pl.ANY)],
        out_specs=[whole()] * 2,
        compiler_params=params,
    )(place, spread, coef, step_face, ghosts_1)
    everywhere = exchange(filtered, first_out)
    ghosts_2 = lax.ppermute(step_face, DOM, step)
    own = pl.pallas_call(
        own_kernel,
        name="own",
        out_shape=jax.ShapeDtypeStruct((chans, atoms), f32),
        in_specs=[whole(pltpu.SMEM), whole(), whole(), whole(pl.ANY)],
        out_specs=whole(),
        compiler_params=params,
    )(counts, positions, features, filtered)
    early = near * 7 // 8
    field_scratch = [
        pltpu.VMEM((256, max(early, near - early) * atoms), bf16),
        pltpu.VMEM((512, 256), bf16),
        pltpu.VMEM((3, near, atoms), f32),
    ]
    field = pl.pallas_call(
        field_kernel,
        name="field",
        out_shape=jax.ShapeDtypeStruct((early, 4, atoms), f32),
        in_specs=[whole()] * 2 + [whole(pl.ANY)],
        out_specs=whole(),
        scratch_shapes=field_scratch,
        compiler_params=params,
    )(everywhere, gathered, own)
    field = pl.pallas_call(
        rest_kernel,
        name="rest",
        out_shape=jax.ShapeDtypeStruct((chans, atoms), bf16),
        in_specs=[whole()] * 3 + [whole(pl.ANY)],
        out_specs=whole(),
        scratch_shapes=field_scratch,
        compiler_params=params,
    )(everywhere, gathered, field, ghosts_2)
    base, twice = pl.pallas_call(
        short_kernel,
        name="short",
        out_shape=[jax.ShapeDtypeStruct((chans, atoms), f32), jax.ShapeDtypeStruct((chans, 2 * chans), bf16)],
        in_specs=[whole()] * 7 + [whole(pl.ANY)],
        out_specs=[whole()] * 2,
        compiler_params=params,
        cost_estimate=pl.CostEstimate(flops=2 * 256 * 256 * atoms, bytes_accessed=10 * 32 * atoms, transcendentals=256 * atoms),
    )(positions, features, ghosts_1, ghosts_2, own, long_weight, short_weight, field)
    longmsg = swap_parts(field.reshape(near, 4, atoms), NEAR, first_near).reshape(chans, atoms)
    all_atoms = atoms * lax.axis_size(ALL)
    long_scale = long_gain / math.sqrt(total_vec * all_atoms)
    return pl.pallas_call(
        lambda *refs: final_kernel(*refs, long_scale=long_scale),
        name="final",
        out_shape=jax.ShapeDtypeStruct((chans, atoms), bf16),
        in_specs=[whole(pltpu.SMEM)] + [whole()] * 3,
        out_specs=whole(),
        compiler_params=params,
    )(counts, base, longmsg, twice)


def solution(mesh):
    fine = Mesh(mesh.devices.reshape(4, 2, 2, 8, 4), ALL)
    return jax.shard_map(
        local,
        mesh=fine,
        in_specs=(P(None, ALL), P(None, ALL), P(ALL), P(ALL, None), P(), P(), P(), P()),
        out_specs=P(None, ALL),
        check_vma=False,
    )
```
